32 devices in a mesh: blk: 8 (over y, x, core), grp: 4 (over z).
Axes of the slice: x: 2, y: 2, z: 4, core: 2. Of those that a mesh axis runs over, the one named last changes fastest.
Arguments:
- spectra: bfloat16 [2, 64, 4, 4096], P(None, 'blk', None, 'grp'), may hold values from -6 to 6
- quality: int32 [64, 4], P('blk'), may hold values from 0 to 3
- pair_mask: int32 [8, 6, 2, 2], P('blk'), may hold values 0 or 1
- owners: int32 [3072, 1], P('blk'), may hold values from 0 to 7; in each aligned block of 384 rows (0 to 383, 384 to 767, ...) at most 96 rows name the same one
- local_rows: int32 [3072], P('blk'), may hold values from 0 to 15
Outputs:
- stack: float32 [128, 2048], P('blk', 'grp')
The draws below stay inside these ranges and needn't reach their ends.
Inputs may be any that keep to these rules, and one draw needn't show every extreme that they name: `owners`: among the rows of one block no owner is named more than 96 times, a bound that some block reaches.
All inputs are finite; a program needn't handle non-finite values. No bound on the sum of `pair_mask` on one device may be relied on, other than what follows from the above.
Results may differ from the reference program's by a relative error of at most 0.0033.
Values may be sent and summed in bfloat16 or wider, within the bound.
No kernel may reach another device: no remote copies, remote signals or barrier semaphores. Data moves between devices by JAX's collectives and lax.ppermute only.
A program may use at most 128 MiB of HBM per device.

```python
import math
import jax
import jax.numpy as jnp
import numpy as np
from jax import lax

STA = 8
WIN = 4
BINS = 4096
LAGS = 2048
STEPS = 6
SUB = 4
VS_DEV = 16
BLOCKS = 8
NSTA = 64
NSB = 2
ROWS = 384
ROWS_ALL = 3072
CAP = 96
VS_TOTAL = 128


def with_ends(entries, key, low, largest):
    longest = entries.shape.index(max(entries.shape))
    spots = []
    for shift in (0, 1):
        where = [jax.random.randint(jax.random.fold_in(key, axis), (), 0, length) for axis, length in enumerate(entries.shape)]
        where[longest] = (where[longest] + shift) % entries.shape[longest]
        spots.append(tuple(where))
    return entries.at[spots[0]].set(low).at[spots[1]].set(largest)


def steps_of(key, extent, cuts, least, largest):
    def one(dim, shards_of):
        steps = jax.random.uniform(jax.random.fold_in(jax.random.fold_in(key, 6), dim), (shards_of,), jnp.float32, least / len(cuts), largest / len(cuts))
        return jnp.repeat(jnp.exp(steps), extent[dim] // shards_of).reshape((-1,) + (1,) * (len(extent) - dim - 1))

    loudness = one(*cuts[0])
    for cut in cuts[1:]:
        loudness = loudness * one(*cut)
    return loudness


def deal_out(own_key, own, number, rows, count, top, limit, lean):
    ranking = jax.random.permutation(own_key, count)
    packed, common = shares(count, rows * top, limit, lean, True), shares(count, rows * top, limit, lean, False)
    places = jnp.arange(count)

    def named(sizes, turn):
        used = int((sizes > 0).sum())
        fixed = max(1, used // 4)
        moved = fixed + (places - fixed + turn * (used - fixed)) % max(1, count - fixed)
        return jnp.zeros((count,), jnp.int32).at[ranking[jnp.where(places < fixed, places, moved)]].set(jnp.asarray(sizes, jnp.int32))

    sizes = jnp.where(number % 4 == 0, named(packed, number // 4), named(common, number - number // 4 - 1))
    mixed = jax.random.permutation(jax.random.fold_in(own, 3), count)
    giver, receiver = mixed[0:count // 2 * 2:2], mixed[1:count // 2 * 2:2]
    margin = jnp.minimum(sizes[giver] - 1, limit - sizes[receiver]) // 2
    margin = jnp.where((giver == ranking[0]) | (receiver == ranking[0]) | (sizes[receiver] == 0), 0, jnp.maximum(margin, 0))
    moved = jax.random.randint(jax.random.fold_in(own, 4), (count // 2,), 0, 1 << 20) % (margin + 1)
    sizes = sizes.at[giver].add(-moved).at[receiver].add(moved)
    labels = jnp.searchsorted(jnp.cumsum(sizes), jnp.arange(rows * top), side="right").astype(jnp.int32)
    listing = labels.reshape(top, rows).T
    listing = listing[jax.random.permutation(jax.random.fold_in(own, 1), rows)]
    turn = jax.random.randint(jax.random.fold_in(own, 2), (rows, 1), 0, top)
    return jnp.take_along_axis(listing, (jnp.arange(top)[None, :] + turn) % top, axis=1)


def shares(amount, total, bound, slope, full):
    portions = [(1 << 20) // math.isqrt(rank ** slope) + 1 for rank in range(1, amount + 1)]
    largest = bound if full else min(bound, max(-(-total // amount), total * portions[0] // sum(portions)))
    least = 1 if total - largest >= amount - 1 else 0
    holding, surplus = [largest] + [least] * (amount - 1), total - largest - least * (amount - 1)
    while surplus > 0:
        candidates = [i for i in range(1, amount) if holding[i] < largest] or [i for i in range(1, amount) if holding[i] < bound]
        whole, budget = sum([portions[i] for i in candidates]), surplus
        for i in candidates:
            addition = min(bound - holding[i], max(1, budget * portions[i] // whole), surplus)
            holding[i] = holding[i] + addition
            surplus = surplus - addition
    return np.array(holding)


def scatter_about(rng, extent, scale, bound, shards=(), kind=jnp.bfloat16):
    level = steps_of(rng, extent, shards, -0.22, 0.18) if shards else 1.0
    result = jax.random.normal(rng, extent, jnp.float32) * scale * level
    return jnp.minimum(jnp.maximum(result, -bound), bound).astype(kind)


def setup_inputs(seed: int = 0) -> dict:
    key_of = jax.random.split(jax.random.key(seed), 6)
    spectra = scatter_about(key_of[0], (2, NSTA, WIN, BINS), 1.0, 6.0, ((1, 8), (3, 4)))
    quality = with_ends(jax.random.randint(key_of[1], (NSTA, WIN), 0, 4), jax.random.fold_in(key_of[1], 1), 0, 3).astype(jnp.int32)
    pair_mask = with_ends((jax.random.randint(key_of[2], (BLOCKS, STEPS, NSB, NSB), 0, 4) < 3).astype(jnp.int32), jax.random.fold_in(key_of[2], 1), 0, 1)
    owners_keys = jax.random.split(jax.random.fold_in(key_of[3], 1), ROWS_ALL // ROWS)
    owners_turns = jax.random.permutation(jax.random.fold_in(key_of[3], 3), ROWS_ALL // ROWS)
    owners = jax.vmap(lambda own, number: deal_out(jax.random.fold_in(key_of[3], 2), own, number, ROWS, BLOCKS, 1, CAP, 2))(owners_keys, owners_turns).reshape((ROWS_ALL, 1))
    local_rows = with_ends(jax.random.randint(key_of[4], (ROWS_ALL,), 0, VS_DEV), jax.random.fold_in(key_of[4], 1), 0, VS_DEV - 1).astype(jnp.int32)
    return {"spectra": spectra, "quality": quality, "pair_mask": pair_mask, "owners": owners, "local_rows": local_rows}


def lag_table(bins_index, total_bins, lags):
    shifts = jnp.arange(lags, dtype=jnp.int32) - lags // 2
    phase = jnp.mod(bins_index[:, None] * shifts[None, :], 2 * total_bins)
    angle = phase.astype(jnp.float32) * (math.pi / total_bins)
    factor = 1.0 / math.sqrt(total_bins)
    return jnp.concatenate([jnp.cos(angle) * factor, -jnp.sin(angle) * factor], axis=0).astype(jnp.bfloat16)

def phase_rows(own_spec, own_weight, far_spec, far_weight, sub_mask):
    near_weight = own_weight.astype(jnp.float32)[:, :, None]
    away_weight = far_weight.astype(jnp.float32)[:, :, None]
    a_real = own_spec[0].astype(jnp.float32) * near_weight
    a_imag = own_spec[1].astype(jnp.float32) * near_weight
    b_real = far_spec[0].astype(jnp.float32) * away_weight
    b_imag = far_spec[1].astype(jnp.float32) * away_weight
    cross_real = lax.optimization_barrier(jnp.sum(a_real[:, None] * b_real[None] + a_imag[:, None] * b_imag[None], axis=2))
    cross_imag = lax.optimization_barrier(jnp.sum(a_imag[:, None] * b_real[None] - a_real[:, None] * b_imag[None], axis=2))
    station_mask = jnp.repeat(jnp.repeat(sub_mask, SUB, axis=0), SUB, axis=1).astype(jnp.float32)
    factor = station_mask[:, :, None] * lax.rsqrt(jnp.maximum(cross_real * cross_real + cross_imag * cross_imag, 1.0))
    joined = jnp.concatenate([cross_real * factor, cross_imag * factor], axis=2).astype(jnp.bfloat16)
    return joined.reshape(STA * STA, joined.shape[2])

def reference(spectra, quality, pair_mask, owners, local_rows):
    owner_flat = owners[:, 0]

    def per_block(carry, block):
        own_spec = lax.dynamic_slice_in_dim(spectra, block * STA, STA, 1)
        own_weight = lax.dynamic_slice_in_dim(quality, block * STA, STA, 0)
        masks = lax.dynamic_index_in_dim(pair_mask, block, 0, keepdims=False)
        pieces = []
        for offset in range(STEPS):
            partner = jnp.mod(block - 1 - offset, BLOCKS).astype(jnp.int32)
            far_spec = lax.dynamic_slice_in_dim(spectra, partner * STA, STA, 1)
            far_weight = lax.dynamic_slice_in_dim(quality, partner * STA, STA, 0)
            pieces.append(phase_rows(own_spec, own_weight, far_spec, far_weight, masks[offset]))
        rows_all = jnp.concatenate(pieces, axis=0)
        first = (block * ROWS).astype(jnp.int32)
        target = lax.dynamic_slice_in_dim(owner_flat, first, ROWS) * VS_DEV + lax.dynamic_slice_in_dim(local_rows, first, ROWS)
        carry = carry.at[target].add(rows_all.astype(jnp.float32))
        return (carry, None)
    start_stack = jnp.zeros((VS_TOTAL, 2 * BINS), jnp.float32)
    binstack, unused = lax.scan(per_block, start_stack, jnp.arange(BLOCKS, dtype=jnp.int32))
    table = lag_table(jnp.arange(BINS, dtype=jnp.int32), BINS, LAGS).astype(jnp.float32)
    return jnp.dot(binstack, table, precision=lax.Precision.HIGHEST, preferred_element_type=jnp.float32)
```

```python
import functools
import math

import jax
import jax.numpy as jnp
import numpy as np
from jax import lax
from jax.experimental import pallas as pl
from jax.experimental.pallas import tpu as pltpu
from jax.sharding import PartitionSpec as P

STA = 8
WIN = 4
BINS = 4096
LAGS = 2048
STEPS = 6
SUB = 4
VS_DEV = 16
LANES = 128
SPEC_ROWS = 2 * WIN * STA
META_ROWS = 16

VMEM = pl.BlockSpec(memory_space=pltpu.VMEM)


def pack_kernel(spec_ref, weight_ref, mask_ref, owner_ref, local_ref, out_ref, plain):
    dests = out_ref.shape[0]
    for part in range(2):
        for station in range(STA):
            first = part * STA * WIN + station * WIN
            values = spec_ref[part, station].astype(jnp.float32)
            for dest in range(dests):
                plain[dest, first : first + WIN, :] = values[:, dest * LANES : (dest + 1) * LANES]
    for dest in range(dests):
        for part in range(2):
            for window in range(0, WIN, 2):
                pair = [
                    plain[dest, pl.ds(part * STA * WIN + window + more, STA, stride=WIN), :]
                    for more in range(2)
                ]
                first = part * STA * WIN + window * STA
                out_ref[dest, first : first + 2 * STA, :] = jnp.concatenate(pair, axis=0).astype(
                    jnp.bfloat16
                )
    lane = lax.broadcasted_iota(jnp.int32, (1, LANES), 1)
    owners, locals_ = [], []
    for chunk in range(STEPS // 2):
        part = slice(chunk * LANES, (chunk + 1) * LANES)
        mask = jnp.zeros((1, LANES), jnp.int32)
        for odd in range(2):
            for near in range(2):
                for far in range(2):
                    here = (lane // 64 == odd) & (lane % 64 // 32 == near) & (lane % 8 // 4 == far)
                    step = chunk * 2 + odd
                    mask = jnp.where(here, mask_ref[near, far : far + 1, step : step + 1], mask)
        owners.append(jnp.where(mask != 0, owner_ref[:, part], -1))
        locals_.append(local_ref[:, part])
    labels = jnp.concatenate(owners + locals_ + [jnp.zeros((2, LANES), jnp.int32)], axis=0)
    station_of = lax.broadcasted_iota(jnp.int32, (STA, STA), 0)
    on_lane = lax.broadcasted_iota(jnp.int32, (STA, STA), 1)
    wide = lax.broadcasted_iota(jnp.int32, (STA, LANES), 1)
    weights = jnp.zeros((STA, LANES), jnp.float32)
    for window in range(WIN):
        row = weight_ref[window : window + 1, :].astype(jnp.float32)
        column = jnp.sum(jnp.where(station_of == on_lane, row, 0.0), axis=1, keepdims=True)
        weights = jnp.where(wide == window, column, weights)
    meta = jnp.concatenate([labels.astype(jnp.float32), weights], axis=0).astype(jnp.bfloat16)
    for dest in range(dests):
        out_ref[dest, SPEC_ROWS:, :] = meta


def pack(spectra, quality, pair_mask, owners, local_rows, blocks):
    rows = owners.shape[0]
    return pl.pallas_call(
        pack_kernel,
        out_shape=jax.ShapeDtypeStruct((blocks, SPEC_ROWS + META_ROWS, LANES), jnp.bfloat16),
        in_specs=[VMEM] * 5,
        out_specs=VMEM,
        scratch_shapes=[pltpu.VMEM((blocks, SPEC_ROWS, LANES), jnp.float32)],
    )(
        spectra,
        quality.T,
        pair_mask[0].transpose(1, 2, 0),
        owners.reshape(1, rows),
        local_rows.reshape(1, rows),
    )


def pair_kernel(got_ref, out_ref, spec, phat, total):
    blocks = got_ref.shape[0]
    groups = out_ref.shape[0] // blocks
    sources = total.shape[0]

    def weigh(block, carry):
        weights = got_ref[block, SPEC_ROWS : SPEC_ROWS + META_ROWS, :].astype(jnp.float32)[STA:]
        for first in range(0, SPEC_ROWS, 2 * STA):
            both = got_ref[block, first : first + 2 * STA, :].astype(jnp.float32)
            for more in range(2):
                place = first // STA + more
                window = place % WIN
                column = weights[:, window : window + 1]
                spec[block, place] = both[more * STA : (more + 1) * STA] * column
        return carry

    lax.fori_loop(0, blocks, weigh, 0)
    total[...] = jnp.zeros_like(total)
    source = lax.broadcasted_iota(jnp.int32, (sources, LANES), 0)

    def correlate(block, carry):
        for near in range(0, STA, 2):
            own = [
                [
                    jnp.broadcast_to(spec[block, place, near + more : near + more + 1, :], (STA, LANES))
                    for place in range(2 * WIN)
                ]
                for more in range(2)
            ]
            for step in range(STEPS):
                far_block = lax.rem(block - 1 - step + blocks, blocks)
                far = [spec[far_block, place] for place in range(2 * WIN)]
                rows = []
                for more in range(2):
                    real, imag = 0.0, 0.0
                    for window in range(WIN):
                        a_real, a_imag = own[more][window], own[more][WIN + window]
                        b_real, b_imag = far[window], far[WIN + window]
                        real += a_real * b_real + a_imag * b_imag
                        imag += a_imag * b_real - a_real * b_imag
                    factor = lax.rsqrt(jnp.maximum(real * real + imag * imag, 1.0))
                    rows.append((real * factor, imag * factor))
                at = step * STA * STA + near * STA
                for part in range(2):
                    tile = jnp.concatenate([rows[0][part], rows[1][part]], axis=0)
                    phat[at : at + 2 * STA, part * LANES : (part + 1) * LANES] = tile.astype(jnp.bfloat16)
        names = got_ref[block, SPEC_ROWS : SPEC_ROWS + META_ROWS, :].astype(jnp.float32).astype(jnp.int32)
        hots = []
        for chunk in range(STEPS // 2):
            label = names[chunk : chunk + 1] * VS_DEV + names[3 + chunk : 4 + chunk]
            label = jnp.where(names[chunk : chunk + 1] < 0, -1, label)
            hots.append((source == label).astype(jnp.bfloat16))
        hot = jnp.concatenate(hots, axis=1)
        total[...] += jnp.dot(hot, phat[...], preferred_element_type=jnp.float32)
        return carry

    lax.fori_loop(0, blocks, correlate, 0)
    for block in range(blocks):
        rows = total[block * VS_DEV : (block + 1) * VS_DEV, :].astype(jnp.bfloat16)
        for group in range(groups):
            out_ref[block * groups + group] = rows


def pairs(got, groups):
    blocks = got.shape[0]
    return pl.pallas_call(
        pair_kernel,
        out_shape=jax.ShapeDtypeStruct((blocks * groups, VS_DEV, 2 * LANES), jnp.bfloat16),
        in_specs=[VMEM],
        out_specs=VMEM,
        scratch_shapes=[
            pltpu.VMEM((blocks, 2 * WIN, STA, LANES), jnp.float32),
            pltpu.VMEM((STEPS * STA * STA, 2 * LANES), jnp.bfloat16),
            pltpu.VMEM((blocks * VS_DEV, 2 * LANES), jnp.float32),
        ],
    )(got)


def lag_kernel(bins_ref, wave_ref, turn_ref, out_ref, lags):
    chunks = bins_ref.shape[0]
    half = out_ref.shape[1]
    rows = bins_ref[...].reshape(chunks * VS_DEV, 2 * LANES)
    for column in range(0, 2 * half, 256):
        part = slice(column, column + 256)
        lags[:, part] = jnp.dot(rows, wave_ref[0, :, part], preferred_element_type=jnp.float32) + jnp.dot(
            rows, wave_ref[1, :, part], preferred_element_type=jnp.float32
        )
    out_ref[...] = jnp.zeros_like(out_ref)

    def add(chunk, carry):
        at = pl.ds(pl.multiple_of(chunk * VS_DEV, VS_DEV), VS_DEV)
        cosine, sine = turn_ref[0, pl.ds(chunk, 1), :], turn_ref[1, pl.ds(chunk, 1), :]
        out_ref[...] += lags[at, :half] * cosine - lags[at, half:] * sine
        return carry

    lax.fori_loop(0, chunks, add, 0)


def lags_of(bins, wave, turn):
    half = wave.shape[2] // 2
    return pl.pallas_call(
        lag_kernel,
        out_shape=jax.ShapeDtypeStruct((VS_DEV, half), jnp.float32),
        in_specs=[VMEM] * 3,
        out_specs=VMEM,
        scratch_shapes=[pltpu.VMEM((bins.shape[0] * VS_DEV, 2 * half), jnp.float32)],
    )(bins, wave, turn)


def wave_table(first_lag, lag_dev):
    bins = jnp.arange(LANES, dtype=jnp.int32)
    shifts = first_lag + jnp.arange(lag_dev, dtype=jnp.int32)
    phase = jnp.mod(bins[:, None] * shifts[None, :], 2 * BINS)
    angle = phase.astype(jnp.float32) * (math.pi / BINS)
    cosine, sine = jnp.cos(angle) / math.sqrt(BINS), jnp.sin(angle) / math.sqrt(BINS)
    full = jnp.concatenate(
        [jnp.concatenate([cosine, sine], axis=1), jnp.concatenate([-sine, cosine], axis=1)], axis=0
    )
    high = full.astype(jnp.bfloat16)
    low = (full - high.astype(jnp.float32)).astype(jnp.bfloat16)
    return jnp.stack([high, low])


def turn_table(first_lag, lag_dev, blocks, groups):
    places = jnp.arange(blocks * groups, dtype=jnp.int32)
    chunk = places % groups * blocks + places // groups
    shifts = first_lag + jnp.arange(lag_dev, dtype=jnp.int32)
    phase = jnp.mod(LANES * chunk[:, None] * shifts[None, :], 2 * BINS)
    angle = phase.astype(jnp.float32) * (math.pi / BINS)
    return jnp.stack([jnp.cos(angle), jnp.sin(angle)])


def by_bins(spectra, quality, pair_mask, owners, local_rows):
    blocks, groups = lax.axis_size("blk"), lax.axis_size("grp")
    lag_dev = LAGS // groups
    first_lag = lax.axis_index("grp") * lag_dev - LAGS // 2
    wave = wave_table(first_lag, lag_dev)
    turn = turn_table(first_lag, lag_dev, blocks, groups)
    sent = pack(spectra, quality, pair_mask, owners, local_rows, blocks)
    got = lax.all_to_all(sent, "blk", split_axis=0, concat_axis=0, tiled=True)
    summed = pairs(got, groups)
    bins = lax.all_to_all(summed, ("blk", "grp"), split_axis=0, concat_axis=0, tiled=True)
    return lags_of(bins, wave, turn)


def from_behind(array, axis, by):
    size = lax.axis_size(axis)
    return lax.ppermute(array, axis, [(i, (i + by) % size) for i in range(size)])


def lag_table(bins_index, total_bins, lags):
    shifts = jnp.arange(lags, dtype=jnp.int32) - lags // 2
    phase = jnp.mod(bins_index[:, None] * shifts[None, :], 2 * total_bins)
    angle = phase.astype(jnp.float32) * (math.pi / total_bins)
    factor = 1.0 / math.sqrt(total_bins)
    return jnp.concatenate([jnp.cos(angle) * factor, -jnp.sin(angle) * factor], axis=0).astype(
        jnp.bfloat16
    )


def phase_rows(own_spec, own_weight, far_spec, far_weight, sub_mask):
    near_weight = own_weight.astype(jnp.float32)[:, :, None]
    away_weight = far_weight.astype(jnp.float32)[:, :, None]
    a_real = own_spec[0].astype(jnp.float32) * near_weight
    a_imag = own_spec[1].astype(jnp.float32) * near_weight
    b_real = far_spec[0].astype(jnp.float32) * away_weight
    b_imag = far_spec[1].astype(jnp.float32) * away_weight
    cross_real = jnp.sum(a_real[:, None] * b_real[None] + a_imag[:, None] * b_imag[None], axis=2)
    cross_imag = jnp.sum(a_imag[:, None] * b_real[None] - a_real[:, None] * b_imag[None], axis=2)
    station_mask = jnp.repeat(jnp.repeat(sub_mask, SUB, axis=0), SUB, axis=1).astype(jnp.float32)
    factor = station_mask[:, :, None] * lax.rsqrt(
        jnp.maximum(cross_real * cross_real + cross_imag * cross_imag, 1.0)
    )
    joined = jnp.concatenate([cross_real * factor, cross_imag * factor], axis=2).astype(
        jnp.bfloat16
    )
    return joined.reshape(STA * STA, joined.shape[2])


def by_halo(spectra, quality, pair_mask, owners, local_rows):
    bins_dev = spectra.shape[3]
    blocks = lax.axis_size("blk")
    rows_dev = owners.shape[0]
    capacity = max(2, 2 * rows_dev // blocks)
    masks = pair_mask[0]
    pieces = [None] * STEPS
    visiting = (spectra, quality)
    for offset in range(STEPS):
        visiting = from_behind((visiting[0], visiting[1]), "blk", 1)
        pieces[offset] = phase_rows(spectra, quality, visiting[0], visiting[1], masks[offset])
    rows_all = jnp.concatenate(pieces, axis=0)
    owner_flat = owners[:, 0]
    row_index = jnp.arange(rows_dev, dtype=jnp.int32)
    earlier = (owner_flat[:, None] == owner_flat[None, :]) & (
        row_index[None, :] < row_index[:, None]
    )
    position = jnp.sum(earlier.astype(jnp.int32), axis=1)
    slot_index = owner_flat * capacity + position
    sources = jnp.arange(VS_DEV, dtype=jnp.int32)
    bins_index = lax.axis_index("grp") * bins_dev + jnp.arange(bins_dev, dtype=jnp.int32)
    table = lag_table(bins_index, BINS, LAGS)
    lag_dev = LAGS // lax.axis_size("grp")
    lag_terms = lax.psum_scatter(
        lax.dot_general(
            table, rows_all, (((0,), (1,)), ((), ())), preferred_element_type=jnp.float32
        ),
        "grp",
        scatter_dimension=0,
        tiled=True,
    )
    outgoing = jnp.zeros((lag_dev, blocks * capacity), jnp.float32).at[:, slot_index].set(lag_terms)
    labels = jnp.full((1, blocks * capacity), -1, jnp.int32).at[0, slot_index].set(local_rows)
    received, got_labels = (
        lax.all_to_all(outgoing, "blk", split_axis=1, concat_axis=1, tiled=True),
        lax.all_to_all(labels, "blk", split_axis=1, concat_axis=1, tiled=True),
    )
    selector = (got_labels == sources[:, None]).astype(jnp.float32)
    stack = lax.dot_general(
        selector,
        received,
        (((1,), (1,)), ((), ())),
        precision=lax.Precision.HIGHEST,
        preferred_element_type=jnp.float32,
    )
    return stack


def on_device(spectra, quality, pair_mask, owners, local_rows):
    if spectra.shape[3] == lax.axis_size("blk") * LANES:
        return by_bins(spectra, quality, pair_mask, owners, local_rows)
    return by_halo(spectra, quality, pair_mask, owners, local_rows)


def solution(mesh):
    in_specs = (
        P(None, "blk", None, "grp"),
        P("blk", None),
        P("blk", None, None, None),
        P("blk", None),
        P("blk"),
    )
    out_specs = P("blk", "grp")
    return jax.shard_map(
        on_device, mesh=mesh, in_specs=in_specs, out_specs=out_specs, check_vma=False
    )
```

```python
import functools
import math

import jax
import jax.numpy as jnp
import numpy as np
from jax import lax
from jax.experimental import pallas as pl
from jax.experimental.pallas import tpu as pltpu
from jax.sharding import PartitionSpec as P

STA = 8
WIN = 4
BINS = 4096
LAGS = 2048
STEPS = 6
SUB = 4
VS_DEV = 16
LANES = 128
SPEC_ROWS = 2 * WIN * STA
META_ROWS = 16
KERNEL_VMEM = 12 * 1024 * 1024

VMEM = pl.BlockSpec(memory_space=pltpu.VMEM)


def pack_kernel(spec_hbm, weight_hbm, mask_hbm, owner_hbm, local_hbm, out_ref, spec_ref, weight_ref, mask_ref, owner_ref, local_ref, plain, arrived):
    dests = out_ref.shape[0]
    moves = [
        pltpu.make_async_copy(source, target, arrived.at[place])
        for place, (source, target) in enumerate(
            [
                (spec_hbm, spec_ref),
                (weight_hbm, weight_ref),
                (mask_hbm, mask_ref),
                (owner_hbm, owner_ref),
                (local_hbm, local_ref),
            ]
        )
    ]
    for move in moves:
        move.start()
    for move in moves:
        move.wait()
    for part in range(2):
        for station in range(STA):
            first = part * STA * WIN + station * WIN
            values = spec_ref[part, station].astype(jnp.float32)
            for dest in range(dests):
                plain[dest, first : first + WIN, :] = values[:, dest * LANES : (dest + 1) * LANES]
    for dest in range(dests):
        for part in range(2):
            for window in range(0, WIN, 2):
                pair = [
                    plain[dest, pl.ds(part * STA * WIN + window + more, STA, stride=WIN), :]
                    for more in range(2)
                ]
                first = part * STA * WIN + window * STA
                out_ref[dest, first : first + 2 * STA, :] = jnp.concatenate(pair, axis=0).astype(
                    jnp.bfloat16
                )
    lane = lax.broadcasted_iota(jnp.int32, (1, LANES), 1)
    owners, locals_ = [], []
    for chunk in range(STEPS // 2):
        part = slice(chunk * LANES, (chunk + 1) * LANES)
        mask = jnp.zeros((1, LANES), jnp.int32)
        for odd in range(2):
            for near in range(2):
                for far in range(2):
                    here = (lane // 64 == odd) & (lane % 64 // 32 == near) & (lane % 8 // 4 == far)
                    step = chunk * 2 + odd
                    mask = jnp.where(here, mask_ref[near, far : far + 1, step : step + 1], mask)
        owners.append(jnp.where(mask != 0, owner_ref[:, part], -1))
        locals_.append(local_ref[part].reshape(1, LANES))
    labels = jnp.concatenate(owners + locals_ + [jnp.zeros((2, LANES), jnp.int32)], axis=0)
    station_of = lax.broadcasted_iota(jnp.int32, (STA, STA), 0)
    on_lane = lax.broadcasted_iota(jnp.int32, (STA, STA), 1)
    wide = lax.broadcasted_iota(jnp.int32, (STA, LANES), 1)
    weights = jnp.zeros((STA, LANES), jnp.float32)
    for window in range(WIN):
        row = weight_ref[window : window + 1, :].astype(jnp.float32)
        column = jnp.sum(jnp.where(station_of == on_lane, row, 0.0), axis=1, keepdims=True)
        weights = jnp.where(wide == window, column, weights)
    meta = jnp.concatenate([labels.astype(jnp.float32), weights], axis=0).astype(jnp.bfloat16)
    for dest in range(dests):
        out_ref[dest, SPEC_ROWS:, :] = meta


def pack(spectra, quality, pair_mask, owners, local_rows, blocks):
    rows = owners.shape[0]
    operands = (
        spectra,
        quality.T,
        pair_mask[0].transpose(1, 2, 0),
        owners.reshape(1, rows),
        local_rows,
    )
    return pl.pallas_call(
        pack_kernel,
        out_shape=pltpu.VMEM((blocks, SPEC_ROWS + META_ROWS, LANES), jnp.bfloat16),
        in_specs=[pl.BlockSpec(memory_space=pltpu.HBM)] * len(operands),
        out_specs=VMEM,
        compiler_params=pltpu.CompilerParams(vmem_limit_bytes=KERNEL_VMEM),
        scratch_shapes=[pltpu.VMEM(each.shape, each.dtype) for each in operands]
        + [
            pltpu.VMEM((blocks, SPEC_ROWS, LANES), jnp.float32),
            pltpu.SemaphoreType.DMA((len(operands),)),
        ],
    )(*[pltpu.with_memory_space_constraint(each, pltpu.HBM) for each in operands])


def pair_kernel(got_ref, out_ref, spec, phat, total):
    blocks = got_ref.shape[0]
    groups = out_ref.shape[0] // blocks
    sources = total.shape[0]

    def weigh(block, carry):
        weights = got_ref[block, SPEC_ROWS : SPEC_ROWS + META_ROWS, :].astype(jnp.float32)[STA:]
        for first in range(0, SPEC_ROWS, 2 * STA):
            both = got_ref[block, first : first + 2 * STA, :].astype(jnp.float32)
            for more in range(2):
                place = first // STA + more
                window = place % WIN
                column = weights[:, window : window + 1]
                spec[block, place] = both[more * STA : (more + 1) * STA] * column
        return carry

    lax.fori_loop(0, blocks, weigh, 0)
    total[...] = jnp.zeros_like(total)
    source = lax.broadcasted_iota(jnp.int32, (sources, LANES), 0)

    def correlate(block, carry):
        for near in range(0, STA, 2):
            own = [
                [
                    jnp.broadcast_to(spec[block, place, near + more : near + more + 1, :], (STA, LANES))
                    for place in range(2 * WIN)
                ]
                for more in range(2)
            ]
            for step in range(STEPS):
                far_block = lax.rem(block - 1 - step + blocks, blocks)
                far = [spec[far_block, place] for place in range(2 * WIN)]
                rows = []
                for more in range(2):
                    real, imag = 0.0, 0.0
                    for window in range(WIN):
                        a_real, a_imag = own[more][window], own[more][WIN + window]
                        b_real, b_imag = far[window], far[WIN + window]
                        real += a_real * b_real + a_imag * b_imag
                        imag += a_imag * b_real - a_real * b_imag
                    factor = lax.rsqrt(jnp.maximum(real * real + imag * imag, 1.0))
                    rows.append((real * factor, imag * factor))
                at = step * STA * STA + near * STA
                for part in range(2):
                    tile = jnp.concatenate([rows[0][part], rows[1][part]], axis=0)
                    phat[at : at + 2 * STA, part * LANES : (part + 1) * LANES] = tile.astype(jnp.bfloat16)
        names = got_ref[block, SPEC_ROWS : SPEC_ROWS + META_ROWS, :].astype(jnp.float32).astype(jnp.int32)
        hots = []
        for chunk in range(STEPS // 2):
            label = names[chunk : chunk + 1] * VS_DEV + names[3 + chunk : 4 + chunk]
            label = jnp.where(names[chunk : chunk + 1] < 0, -1, label)
            hots.append((source == label).astype(jnp.bfloat16))
        hot = jnp.concatenate(hots, axis=1)
        total[...] += jnp.dot(hot, phat[...], preferred_element_type=jnp.float32)
        return carry

    lax.fori_loop(0, blocks, correlate, 0)
    for block in range(blocks):
        rows = total[block * VS_DEV : (block + 1) * VS_DEV, :].astype(jnp.bfloat16)
        for group in range(groups):
            out_ref[block * groups + group] = rows


def pairs(got, groups):
    blocks = got.shape[0]
    return pl.pallas_call(
        pair_kernel,
        out_shape=pltpu.VMEM((blocks * groups, VS_DEV, 2 * LANES), jnp.bfloat16),
        in_specs=[VMEM],
        out_specs=VMEM,
        compiler_params=pltpu.CompilerParams(vmem_limit_bytes=KERNEL_VMEM),
        scratch_shapes=[
            pltpu.VMEM((blocks, 2 * WIN, STA, LANES), jnp.float32),
            pltpu.VMEM((STEPS * STA * STA, 2 * LANES), jnp.bfloat16),
            pltpu.VMEM((blocks * VS_DEV, 2 * LANES), jnp.float32),
        ],
    )(got)


def lag_kernel(bins_ref, wave_ref, turn_ref, out_ref, lags):
    chunks = bins_ref.shape[0]
    half = out_ref.shape[1]
    rows = bins_ref[...].reshape(chunks * VS_DEV, 2 * LANES)
    for column in range(0, 2 * half, 256):
        part = slice(column, column + 256)
        lags[:, part] = jnp.dot(rows, wave_ref[0, :, part], preferred_element_type=jnp.float32) + jnp.dot(
            rows, wave_ref[1, :, part], preferred_element_type=jnp.float32
        )
    out_ref[...] = jnp.zeros_like(out_ref)

    def add(chunk, carry):
        at = pl.ds(pl.multiple_of(chunk * VS_DEV, VS_DEV), VS_DEV)
        cosine, sine = turn_ref[0, pl.ds(chunk, 1), :], turn_ref[1, pl.ds(chunk, 1), :]
        out_ref[...] += lags[at, :half] * cosine - lags[at, half:] * sine
        return carry

    lax.fori_loop(0, chunks, add, 0)


def lags_of(bins, wave, turn):
    half = wave.shape[2] // 2
    return pl.pallas_call(
        lag_kernel,
        out_shape=jax.ShapeDtypeStruct((VS_DEV, half), jnp.float32),
        in_specs=[VMEM] * 3,
        out_specs=VMEM,
        compiler_params=pltpu.CompilerParams(vmem_limit_bytes=KERNEL_VMEM),
        scratch_shapes=[pltpu.VMEM((bins.shape[0] * VS_DEV, 2 * half), jnp.float32)],
    )(bins, wave, turn)


def wave_table(first_lag, lag_dev):
    bins = jnp.arange(LANES, dtype=jnp.int32)
    shifts = first_lag + jnp.arange(lag_dev, dtype=jnp.int32)
    phase = jnp.mod(bins[:, None] * shifts[None, :], 2 * BINS)
    angle = phase.astype(jnp.float32) * (math.pi / BINS)
    cosine, sine = jnp.cos(angle) / math.sqrt(BINS), jnp.sin(angle) / math.sqrt(BINS)
    full = jnp.concatenate(
        [jnp.concatenate([cosine, sine], axis=1), jnp.concatenate([-sine, cosine], axis=1)], axis=0
    )
    high = full.astype(jnp.bfloat16)
    low = (full - high.astype(jnp.float32)).astype(jnp.bfloat16)
    return jnp.stack([high, low])


def turn_table(first_lag, lag_dev, blocks, groups):
    places = jnp.arange(blocks * groups, dtype=jnp.int32)
    chunk = places % groups * blocks + places // groups
    shifts = first_lag + jnp.arange(lag_dev, dtype=jnp.int32)
    phase = jnp.mod(LANES * chunk[:, None] * shifts[None, :], 2 * BINS)
    angle = phase.astype(jnp.float32) * (math.pi / BINS)
    return jnp.stack([jnp.cos(angle), jnp.sin(angle)])


def by_bins(spectra, quality, pair_mask, owners, local_rows):
    blocks, groups = lax.axis_size("blk"), lax.axis_size("grp")
    lag_dev = LAGS // groups
    first_lag = lax.axis_index("grp") * lag_dev - LAGS // 2
    wave = wave_table(first_lag, lag_dev)
    turn = turn_table(first_lag, lag_dev, blocks, groups)
    sent = pack(spectra, quality, pair_mask, owners, local_rows, blocks)
    got = lax.all_to_all(sent, "blk", split_axis=0, concat_axis=0, tiled=True)
    got, wave, turn = lax.optimization_barrier((got, wave, turn))
    summed = pairs(got, groups)
    bins = lax.all_to_all(summed, ("blk", "grp"), split_axis=0, concat_axis=0, tiled=True)
    return lags_of(bins, wave, turn)


def from_behind(array, axis, by):
    size = lax.axis_size(axis)
    return lax.ppermute(array, axis, [(i, (i + by) % size) for i in range(size)])


def lag_table(bins_index, total_bins, lags):
    shifts = jnp.arange(lags, dtype=jnp.int32) - lags // 2
    phase = jnp.mod(bins_index[:, None] * shifts[None, :], 2 * total_bins)
    angle = phase.astype(jnp.float32) * (math.pi / total_bins)
    factor = 1.0 / math.sqrt(total_bins)
    return jnp.concatenate([jnp.cos(angle) * factor, -jnp.sin(angle) * factor], axis=0).astype(
        jnp.bfloat16
    )


def phase_rows(own_spec, own_weight, far_spec, far_weight, sub_mask):
    near_weight = own_weight.astype(jnp.float32)[:, :, None]
    away_weight = far_weight.astype(jnp.float32)[:, :, None]
    a_real = own_spec[0].astype(jnp.float32) * near_weight
    a_imag = own_spec[1].astype(jnp.float32) * near_weight
    b_real = far_spec[0].astype(jnp.float32) * away_weight
    b_imag = far_spec[1].astype(jnp.float32) * away_weight
    cross_real = jnp.sum(a_real[:, None] * b_real[None] + a_imag[:, None] * b_imag[None], axis=2)
    cross_imag = jnp.sum(a_imag[:, None] * b_real[None] - a_real[:, None] * b_imag[None], axis=2)
    station_mask = jnp.repeat(jnp.repeat(sub_mask, SUB, axis=0), SUB, axis=1).astype(jnp.float32)
    factor = station_mask[:, :, None] * lax.rsqrt(
        jnp.maximum(cross_real * cross_real + cross_imag * cross_imag, 1.0)
    )
    joined = jnp.concatenate([cross_real * factor, cross_imag * factor], axis=2).astype(
        jnp.bfloat16
    )
    return joined.reshape(STA * STA, joined.shape[2])


def by_halo(spectra, quality, pair_mask, owners, local_rows):
    bins_dev = spectra.shape[3]
    blocks = lax.axis_size("blk")
    rows_dev = owners.shape[0]
    capacity = max(2, 2 * rows_dev // blocks)
    masks = pair_mask[0]
    pieces = [None] * STEPS
    visiting = (spectra, quality)
    for offset in range(STEPS):
        visiting = from_behind((visiting[0], visiting[1]), "blk", 1)
        pieces[offset] = phase_rows(spectra, quality, visiting[0], visiting[1], masks[offset])
    rows_all = jnp.concatenate(pieces, axis=0)
    owner_flat = owners[:, 0]
    row_index = jnp.arange(rows_dev, dtype=jnp.int32)
    earlier = (owner_flat[:, None] == owner_flat[None, :]) & (
        row_index[None, :] < row_index[:, None]
    )
    position = jnp.sum(earlier.astype(jnp.int32), axis=1)
    slot_index = owner_flat * capacity + position
    sources = jnp.arange(VS_DEV, dtype=jnp.int32)
    bins_index = lax.axis_index("grp") * bins_dev + jnp.arange(bins_dev, dtype=jnp.int32)
    table = lag_table(bins_index, BINS, LAGS)
    lag_dev = LAGS // lax.axis_size("grp")
    lag_terms = lax.psum_scatter(
        lax.dot_general(
            table, rows_all, (((0,), (1,)), ((), ())), preferred_element_type=jnp.float32
        ),
        "grp",
        scatter_dimension=0,
        tiled=True,
    )
    outgoing = jnp.zeros((lag_dev, blocks * capacity), jnp.float32).at[:, slot_index].set(lag_terms)
    labels = jnp.full((1, blocks * capacity), -1, jnp.int32).at[0, slot_index].set(local_rows)
    received, got_labels = (
        lax.all_to_all(outgoing, "blk", split_axis=1, concat_axis=1, tiled=True),
        lax.all_to_all(labels, "blk", split_axis=1, concat_axis=1, tiled=True),
    )
    selector = (got_labels == sources[:, None]).astype(jnp.float32)
    stack = lax.dot_general(
        selector,
        received,
        (((1,), (1,)), ((), ())),
        precision=lax.Precision.HIGHEST,
        preferred_element_type=jnp.float32,
    )
    return stack


def on_device(spectra, quality, pair_mask, owners, local_rows):
    if spectra.shape[3] == lax.axis_size("blk") * LANES:
        return by_bins(spectra, quality, pair_mask, owners, local_rows)
    return by_halo(spectra, quality, pair_mask, owners, local_rows)


def solution(mesh):
    in_specs = (
        P(None, "blk", None, "grp"),
        P("blk", None),
        P("blk", None, None, None),
        P("blk", None),
        P("blk"),
    )
    out_specs = P("blk", "grp")
    return jax.shard_map(
        on_device, mesh=mesh, in_specs=in_specs, out_specs=out_specs, check_vma=False
    )
```

```python
import functools
import math

import jax
import jax.numpy as jnp
import numpy as np
from jax import lax
from jax.experimental import pallas as pl
from jax.experimental.pallas import tpu as pltpu
from jax.sharding import PartitionSpec as P

STA = 8
WIN = 4
BINS = 4096
LAGS = 2048
STEPS = 6
SUB = 4
VS_DEV = 16
LANES = 128
SPEC_ROWS = 2 * WIN * STA
META_ROWS = 16
KERNEL_VMEM = 12 * 1024 * 1024

VMEM = pl.BlockSpec(memory_space=pltpu.VMEM)


def pack_kernel(
    spec_hbm,
    weight_hbm,
    mask_hbm,
    owner_hbm,
    local_hbm,
    out_ref,
    spec_ref,
    weight_ref,
    mask_ref,
    owner_ref,
    local_ref,
    plain,
    arrived,
):
    dests = out_ref.shape[0]
    moves = [
        pltpu.make_async_copy(source, target, arrived.at[place])
        for place, (source, target) in enumerate(
            [
                (spec_hbm, spec_ref),
                (weight_hbm, weight_ref),
                (mask_hbm, mask_ref),
                (owner_hbm, owner_ref),
                (local_hbm, local_ref),
            ]
        )
    ]
    for move in moves:
        move.start()
    lane = lax.broadcasted_iota(jnp.int32, (1, LANES), 1)
    lane_in = lax.broadcasted_iota(jnp.int32, (LANES, LANES), 0)
    lane_out = lax.broadcasted_iota(jnp.int32, (LANES, LANES), 1)
    turned = lane_out // 64 * 64 + lane_out % STA * STA + lane_out % 64 // STA
    swap = (lane_in == turned).astype(jnp.float32).astype(jnp.bfloat16)
    for move in moves:
        move.wait()
    for part in range(2):
        for station in range(STA):
            first = part * STA * WIN + station * WIN
            values = spec_ref[part, station].astype(jnp.float32)
            for dest in range(dests):
                plain[dest, first : first + WIN, :] = values[:, dest * LANES : (dest + 1) * LANES]
    labels = []
    for chunk in range(STEPS // 2):
        part = slice(chunk * LANES, (chunk + 1) * LANES)
        mask = jnp.zeros((1, LANES), jnp.int32)
        for odd in range(2):
            for near in range(2):
                for far in range(2):
                    here = (lane // 64 == odd) & (lane % 64 // 32 == near) & (lane % 8 // 4 == far)
                    step = chunk * 2 + odd
                    mask = jnp.where(here, mask_ref[near, far : far + 1, step : step + 1], mask)
        source = owner_ref[:, part] * VS_DEV + local_ref[part].reshape(1, LANES)
        labels.append(jnp.where(mask != 0, source, -1).astype(jnp.float32))
    last = jnp.broadcast_to(labels[2], (STA, LANES)).astype(jnp.bfloat16)
    labels[2] = jnp.dot(last, swap, preferred_element_type=jnp.float32)[:1]
    station_of = lax.broadcasted_iota(jnp.int32, (STA, STA), 0)
    on_lane = lax.broadcasted_iota(jnp.int32, (STA, STA), 1)
    wide = lax.broadcasted_iota(jnp.int32, (STA, LANES), 1)
    weights = jnp.zeros((STA, LANES), jnp.float32)
    for window in range(WIN):
        row = weight_ref[window : window + 1, :].astype(jnp.float32)
        column = jnp.sum(jnp.where(station_of == on_lane, row, 0.0), axis=1, keepdims=True)
        weights = jnp.where(wide == window, column, weights)
    meta = jnp.concatenate(labels + [jnp.zeros((5, LANES), jnp.float32), weights], axis=0).astype(jnp.bfloat16)
    for dest in range(dests):
        for part in range(2):
            for window in range(0, WIN, 2):
                pair = [
                    plain[dest, pl.ds(part * STA * WIN + window + more, STA, stride=WIN), :]
                    for more in range(2)
                ]
                first = part * STA * WIN + window * STA
                out_ref[dest, first : first + 2 * STA, :] = jnp.concatenate(pair, axis=0).astype(
                    jnp.bfloat16
                )
        out_ref[dest, SPEC_ROWS:, :] = meta


def pack(spectra, quality, pair_mask, owners, local_rows, blocks):
    rows = owners.shape[0]
    operands = (
        spectra,
        quality.T,
        pair_mask[0].transpose(1, 2, 0),
        owners.reshape(1, rows),
        local_rows,
    )
    return pl.pallas_call(
        pack_kernel,
        out_shape=pltpu.VMEM((blocks, SPEC_ROWS + META_ROWS, LANES), jnp.bfloat16),
        in_specs=[pl.BlockSpec(memory_space=pltpu.HBM)] * len(operands),
        out_specs=VMEM,
        compiler_params=pltpu.CompilerParams(vmem_limit_bytes=KERNEL_VMEM),
        scratch_shapes=[pltpu.VMEM(each.shape, each.dtype) for each in operands]
        + [
            pltpu.VMEM((blocks, SPEC_ROWS, LANES), jnp.float32),
            pltpu.SemaphoreType.DMA((len(operands),)),
        ],
    )(*[pltpu.with_memory_space_constraint(each, pltpu.HBM) for each in operands])


def pair_kernel(got_ref, lead_ref, out_ref, spec, phat, hot, total):
    blocks = got_ref.shape[0]
    groups = out_ref.shape[0] // blocks
    sources = blocks * VS_DEV
    kept = STEPS // 2 + 1
    block_rows = kept * STA * STA

    for block in range(blocks):
        weights = got_ref[block, SPEC_ROWS : SPEC_ROWS + META_ROWS, :].astype(jnp.float32)[STA:]
        columns = [weights[:, window : window + 1] for window in range(WIN)]
        for first in range(0, SPEC_ROWS, 2 * STA):
            both = got_ref[block, first : first + 2 * STA, :].astype(jnp.float32)
            for more in range(2):
                place = first // STA + more
                spec[block, place] = both[more * STA : (more + 1) * STA] * columns[place % WIN]

    source = lax.broadcasted_iota(jnp.int32, (sources, LANES), 0).astype(jnp.float32)
    lane = lax.broadcasted_iota(jnp.int32, (1, LANES), 1)

    def earlier(block, by):
        return lax.rem(block - by + blocks, blocks)

    def names(block, chunk):
        rows = got_ref[block, SPEC_ROWS : SPEC_ROWS + META_ROWS, :].astype(jnp.float32)
        return rows[chunk : chunk + 1]

    def correlate(block, carry):
        base = pl.multiple_of(block * block_rows, block_rows)
        for near in range(0, STA, 2):
            own = [
                [
                    jnp.broadcast_to(spec[block, place, near + more : near + more + 1, :], (STA, LANES))
                    for place in range(2 * WIN)
                ]
                for more in range(2)
            ]
            for step in range(kept):
                far_block = earlier(block, 1 + step)
                far = [spec[far_block, place] for place in range(2 * WIN)]
                rows = []
                for more in range(2):
                    real, imag = 0.0, 0.0
                    for window in range(WIN):
                        a_real, a_imag = own[more][window], own[more][WIN + window]
                        b_real, b_imag = far[window], far[WIN + window]
                        real += a_real * b_real + a_imag * b_imag
                        imag += a_imag * b_real - a_real * b_imag
                    factor = lax.rsqrt(jnp.maximum(real * real + imag * imag, 1.0))
                    rows.append((real * factor, imag * factor))
                at = base + (step * STA * STA + near * STA)
                for part in range(2):
                    tile = jnp.concatenate([rows[0][part], rows[1][part]], axis=0)
                    phat[pl.ds(pl.multiple_of(at, 2 * STA), 2 * STA), part * LANES : (part + 1) * LANES] = (
                        tile.astype(jnp.bfloat16)
                    )
        again = [
            jnp.where(lane >= LANES // 2, names(earlier(block, 2), 2), -1.0),
            jnp.where(lane < LANES // 2, names(earlier(block, 3), 2), -1.0),
        ]
        for chunk in range(2):
            forth = (source == names(block, chunk)).astype(jnp.float32)
            back = (source == again[chunk]).astype(jnp.float32)
            at = pl.ds(pl.multiple_of(base + chunk * LANES, LANES), LANES)
            hot[:sources, at] = (forth + back).astype(jnp.bfloat16)
            hot[sources:, at] = (forth - back).astype(jnp.bfloat16)
        return carry

    lax.fori_loop(0, blocks, correlate, 0)
    total[...] = jnp.dot(hot[...], phat[...], preferred_element_type=jnp.float32)
    for block in range(blocks):
        at = slice(block * VS_DEV, (block + 1) * VS_DEV)
        real = total[at, :LANES]
        imag = total[sources + block * VS_DEV : sources + (block + 1) * VS_DEV, LANES:]
        for group in range(groups):
            cosine, sine = lead_ref[group : group + 1, :], lead_ref[groups + group : groups + group + 1, :]
            out_ref[block * groups + group] = jnp.concatenate(
                [real * cosine - imag * sine, real * sine + imag * cosine], axis=1
            ).astype(jnp.bfloat16)


def pairs(got, lead):
    blocks, groups = got.shape[0], lead.shape[0] // 2
    block_rows = (STEPS // 2 + 1) * STA * STA
    return pl.pallas_call(
        pair_kernel,
        out_shape=pltpu.VMEM((blocks * groups, VS_DEV, 2 * LANES), jnp.bfloat16),
        in_specs=[VMEM] * 2,
        out_specs=VMEM,
        compiler_params=pltpu.CompilerParams(vmem_limit_bytes=KERNEL_VMEM),
        scratch_shapes=[
            pltpu.VMEM((blocks, 2 * WIN, STA, LANES), jnp.float32),
            pltpu.VMEM((blocks * block_rows, 2 * LANES), jnp.bfloat16),
            pltpu.VMEM((2 * blocks * VS_DEV, blocks * block_rows), jnp.bfloat16),
            pltpu.VMEM((2 * blocks * VS_DEV, 2 * LANES), jnp.float32),
        ],
    )(got, lead)


def lag_kernel(bins_ref, wave_ref, turn_ref, out_ref):
    chunks = bins_ref.shape[0]
    rows = bins_ref[...].reshape(chunks * VS_DEV, 2 * LANES)
    for tile in range(wave_ref.shape[1]):
        lags = jnp.dot(rows, wave_ref[0, tile], preferred_element_type=jnp.float32) + jnp.dot(
            rows, wave_ref[1, tile], preferred_element_type=jnp.float32
        )
        total = jnp.zeros((VS_DEV, LANES), jnp.float32)
        for chunk in range(chunks):
            piece = lags[chunk * VS_DEV : (chunk + 1) * VS_DEV]
            total += piece[:, :LANES] * turn_ref[0, chunk : chunk + 1, :]
            total -= piece[:, LANES:] * turn_ref[1, chunk : chunk + 1, :]
        out_ref[:, tile * LANES : (tile + 1) * LANES] = total


def lags_of(bins, wave, turn):
    return pl.pallas_call(
        lag_kernel,
        out_shape=jax.ShapeDtypeStruct((VS_DEV, wave.shape[1] * LANES), jnp.float32),
        in_specs=[VMEM] * 3,
        out_specs=VMEM,
        compiler_params=pltpu.CompilerParams(vmem_limit_bytes=KERNEL_VMEM),
    )(bins, wave, turn)


def turns(phase):
    angle = np.mod(phase, 2 * BINS) * (math.pi / BINS)
    return np.cos(angle), np.sin(angle)


def lag_tables(blocks, groups):
    lag_dev = LAGS // groups
    first = np.arange(groups) * lag_dev - LAGS // 2
    bins = np.arange(LANES)
    lead = np.concatenate(turns(first[:, None] * bins[None, :])).astype(np.float32)
    cosine, sine = turns(bins[:, None] * np.arange(lag_dev)[None, :])
    tiles = []
    for at in range(0, lag_dev, LANES):
        part = slice(at, at + LANES)
        tiles.append(np.block([[cosine[:, part], sine[:, part]], [-sine[:, part], cosine[:, part]]]))
    wave = np.stack(tiles) / math.sqrt(BINS)
    high = wave.astype(jnp.bfloat16)
    low = (wave - high.astype(np.float64)).astype(jnp.bfloat16)
    place = np.arange(blocks * groups)
    chunk = place % groups * blocks + place // groups
    turn = np.stack(turns(LANES * chunk[:, None] * bins[None, :])).astype(np.float32)
    return jnp.asarray(lead), jnp.asarray(np.stack([high, low])), jnp.asarray(turn)


def by_bins(spectra, quality, pair_mask, owners, local_rows):
    blocks, groups = lax.axis_size("blk"), lax.axis_size("grp")
    lead, wave, turn = lag_tables(blocks, groups)
    sent = pack(spectra, quality, pair_mask, owners, local_rows, blocks)
    got = lax.all_to_all(sent, "blk", split_axis=0, concat_axis=0, tiled=True)
    summed = pairs(got, lead)
    bins = lax.all_to_all(summed, ("blk", "grp"), split_axis=0, concat_axis=0, tiled=True)
    return lags_of(bins, wave, turn)


def from_behind(array, axis, by):
    size = lax.axis_size(axis)
    return lax.ppermute(array, axis, [(i, (i + by) % size) for i in range(size)])


def lag_table(bins_index, total_bins, lags):
    shifts = jnp.arange(lags, dtype=jnp.int32) - lags // 2
    phase = jnp.mod(bins_index[:, None] * shifts[None, :], 2 * total_bins)
    angle = phase.astype(jnp.float32) * (math.pi / total_bins)
    factor = 1.0 / math.sqrt(total_bins)
    return jnp.concatenate([jnp.cos(angle) * factor, -jnp.sin(angle) * factor], axis=0).astype(
        jnp.bfloat16
    )


def phase_rows(own_spec, own_weight, far_spec, far_weight, sub_mask):
    near_weight = own_weight.astype(jnp.float32)[:, :, None]
    away_weight = far_weight.astype(jnp.float32)[:, :, None]
    a_real = own_spec[0].astype(jnp.float32) * near_weight
    a_imag = own_spec[1].astype(jnp.float32) * near_weight
    b_real = far_spec[0].astype(jnp.float32) * away_weight
    b_imag = far_spec[1].astype(jnp.float32) * away_weight
    cross_real = jnp.sum(a_real[:, None] * b_real[None] + a_imag[:, None] * b_imag[None], axis=2)
    cross_imag = jnp.sum(a_imag[:, None] * b_real[None] - a_real[:, None] * b_imag[None], axis=2)
    station_mask = jnp.repeat(jnp.repeat(sub_mask, SUB, axis=0), SUB, axis=1).astype(jnp.float32)
    factor = station_mask[:, :, None] * lax.rsqrt(
        jnp.maximum(cross_real * cross_real + cross_imag * cross_imag, 1.0)
    )
    joined = jnp.concatenate([cross_real * factor, cross_imag * factor], axis=2).astype(
        jnp.bfloat16
    )
    return joined.reshape(STA * STA, joined.shape[2])


def by_halo(spectra, quality, pair_mask, owners, local_rows):
    bins_dev = spectra.shape[3]
    blocks = lax.axis_size("blk")
    rows_dev = owners.shape[0]
    capacity = max(2, 2 * rows_dev // blocks)
    masks = pair_mask[0]
    pieces = [None] * STEPS
    visiting = (spectra, quality)
    for offset in range(STEPS):
        visiting = from_behind((visiting[0], visiting[1]), "blk", 1)
        pieces[offset] = phase_rows(spectra, quality, visiting[0], visiting[1], masks[offset])
    rows_all = jnp.concatenate(pieces, axis=0)
    owner_flat = owners[:, 0]
    row_index = jnp.arange(rows_dev, dtype=jnp.int32)
    earlier = (owner_flat[:, None] == owner_flat[None, :]) & (
        row_index[None, :] < row_index[:, None]
    )
    position = jnp.sum(earlier.astype(jnp.int32), axis=1)
    slot_index = owner_flat * capacity + position
    sources = jnp.arange(VS_DEV, dtype=jnp.int32)
    bins_index = lax.axis_index("grp") * bins_dev + jnp.arange(bins_dev, dtype=jnp.int32)
    table = lag_table(bins_index, BINS, LAGS)
    lag_dev = LAGS // lax.axis_size("grp")
    lag_terms = lax.psum_scatter(
        lax.dot_general(
            table, rows_all, (((0,), (1,)), ((), ())), preferred_element_type=jnp.float32
        ),
        "grp",
        scatter_dimension=0,
        tiled=True,
    )
    outgoing = jnp.zeros((lag_dev, blocks * capacity), jnp.float32).at[:, slot_index].set(lag_terms)
    labels = jnp.full((1, blocks * capacity), -1, jnp.int32).at[0, slot_index].set(local_rows)
    received, got_labels = (
        lax.all_to_all(outgoing, "blk", split_axis=1, concat_axis=1, tiled=True),
        lax.all_to_all(labels, "blk", split_axis=1, concat_axis=1, tiled=True),
    )
    selector = (got_labels == sources[:, None]).astype(jnp.float32)
    stack = lax.dot_general(
        selector,
        received,
        (((1,), (1,)), ((), ())),
        precision=lax.Precision.HIGHEST,
        preferred_element_type=jnp.float32,
    )
    return stack


def on_device(spectra, quality, pair_mask, owners, local_rows):
    blocks, groups = lax.axis_size("blk"), lax.axis_size("grp")
    whole_tiles = spectra.shape[3] == blocks * LANES and LANES * (LAGS // groups) % (2 * BINS) == 0
    if whole_tiles and blocks == STEPS + 2:
        return by_bins(spectra, quality, pair_mask, owners, local_rows)
    return by_halo(spectra, quality, pair_mask, owners, local_rows)


def solution(mesh):
    in_specs = (
        P(None, "blk", None, "grp"),
        P("blk", None),
        P("blk", None, None, None),
        P("blk", None),
        P("blk"),
    )
    out_specs = P("blk", "grp")
    return jax.shard_map(
        on_device, mesh=mesh, in_specs=in_specs, out_specs=out_specs, check_vma=False
    )
```

```python
import functools
import math

import jax
import jax.numpy as jnp
import numpy as np
from jax import lax
from jax.experimental import pallas as pl
from jax.experimental.pallas import tpu as pltpu
from jax.sharding import PartitionSpec as P

STA = 8
WIN = 4
BINS = 4096
LAGS = 2048
STEPS = 6
SUB = 4
VS_DEV = 16
LANES = 128
SPEC_TILES = 2 * STA
KERNEL_VMEM = 12 * 1024 * 1024

VMEM = pl.BlockSpec(memory_space=pltpu.VMEM)


def pack_kernel(spec_hbm, weight_hbm, mask_hbm, owner_hbm, local_hbm, out_ref, weight_ref, mask_ref, owner_ref, local_ref, sliced, arrived):
    dests = out_ref.shape[0]
    slices = [
        pltpu.make_async_copy(
            spec_hbm.at[:, :, pl.ds(dest * LANES, LANES)],
            out_ref.at[dest, pl.ds(0, SPEC_TILES)],
            sliced.at[dest],
        )
        for dest in range(dests)
    ]
    small = [(weight_hbm, weight_ref), (mask_hbm, mask_ref), (owner_hbm, owner_ref), (local_hbm, local_ref)]
    moves = [
        pltpu.make_async_copy(source, target, arrived.at[place])
        for place, (source, target) in enumerate(small)
    ]
    for move in moves + slices:
        move.start()
    lane = lax.broadcasted_iota(jnp.int32, (1, LANES), 1)
    for move in moves:
        move.wait()
    rows = []
    for chunk in range(STEPS // 2):
        part = slice(chunk * LANES, (chunk + 1) * LANES)
        mask = jnp.zeros((1, LANES), jnp.int32)
        for odd in range(2):
            for near in range(2):
                for far in range(2):
                    here = (lane // 64 == odd) & (lane % 64 // 32 == near) & (lane % 8 // 4 == far)
                    step = chunk * 2 + odd
                    mask = jnp.where(here, mask_ref[near, far : far + 1, step : step + 1], mask)
        source = owner_ref[:, part] * VS_DEV + local_ref[part].reshape(1, LANES)
        rows.append(jnp.where(mask != 0, source, -1).astype(jnp.float32))
    weights = [weight_ref[window : window + 1, :].astype(jnp.float32) for window in range(WIN)]
    rows.append(jnp.concatenate(weights + [jnp.zeros((1, LANES - WIN * STA), jnp.float32)], axis=1))
    meta = jnp.concatenate(rows, axis=0).astype(jnp.bfloat16)
    for dest in range(dests):
        out_ref[dest, SPEC_TILES] = meta
    for move in slices:
        move.wait()


def pack(spectra, quality, pair_mask, owners, local_rows, blocks):
    rows = owners.shape[0]
    operands = (
        spectra.reshape(SPEC_TILES, WIN, spectra.shape[3]),
        quality.T,
        pair_mask[0].transpose(1, 2, 0),
        owners.reshape(1, rows),
        local_rows,
    )
    return pl.pallas_call(
        pack_kernel,
        out_shape=pltpu.VMEM((blocks, SPEC_TILES + 1, WIN, LANES), jnp.bfloat16),
        in_specs=[pl.BlockSpec(memory_space=pltpu.HBM)] * len(operands),
        out_specs=VMEM,
        compiler_params=pltpu.CompilerParams(vmem_limit_bytes=KERNEL_VMEM),
        scratch_shapes=[pltpu.VMEM(each.shape, each.dtype) for each in operands[1:]]
        + [pltpu.SemaphoreType.DMA((blocks,)), pltpu.SemaphoreType.DMA((len(operands) - 1,))],
    )(*[pltpu.with_memory_space_constraint(each, pltpu.HBM) for each in operands])


def pair_kernel(got_ref, lead_hbm, out_ref, lead_ref, plain, meta, own_spec, far_spec, names, phat, hot, total, arrived):
    blocks = got_ref.shape[0]
    groups = out_ref.shape[0] // blocks
    sources = blocks * VS_DEV
    tile_rows = STA * STA
    lead_move = pltpu.make_async_copy(lead_hbm, lead_ref, arrived)
    lead_move.start()

    for block in range(blocks):
        for tile in range(SPEC_TILES):
            plain[block, tile * WIN : (tile + 1) * WIN, :] = got_ref[block, tile].astype(jnp.float32)
        meta[block * WIN : (block + 1) * WIN, :] = got_ref[block, SPEC_TILES].astype(jnp.float32)
    weights = meta[pl.ds(WIN - 1, blocks, stride=WIN), :].T
    for block in range(blocks):
        for window in range(WIN):
            column = weights[window * STA : (window + 1) * STA, block : block + 1]
            real = plain[block, pl.ds(window, STA, stride=WIN), :] * column
            imag = plain[block, pl.ds(STA * WIN + window, STA, stride=WIN), :] * column
            for place, (near, far) in enumerate([(real, real), (imag, imag), (real + imag, real - imag)]):
                own_spec[block, place * WIN + window] = near
                far_spec[block, place * WIN + window] = far

    lane_in = lax.broadcasted_iota(jnp.int32, (LANES, LANES), 0)
    lane_out = lax.broadcasted_iota(jnp.int32, (LANES, LANES), 1)
    turned = lane_out // tile_rows * tile_rows + lane_out % STA * STA + lane_out % tile_rows // STA
    swap = (lane_in == turned).astype(jnp.float32).astype(jnp.bfloat16)
    for chunk in range(STEPS // 2):
        here = meta[pl.ds(chunk, blocks, stride=WIN), :]
        if chunk:
            other = jnp.dot(here.astype(jnp.bfloat16), swap, preferred_element_type=jnp.float32)
            if chunk == 1:
                block_of = lax.broadcasted_iota(jnp.int32, here.shape, 0)
                lane = lax.broadcasted_iota(jnp.int32, here.shape, 1)
                other = jnp.where((block_of >= blocks // 2) & (lane >= tile_rows), other, here)
            here = other
        names[chunk] = here
    source = lax.broadcasted_iota(jnp.int32, (sources, LANES), 0).astype(jnp.float32)
    for block in range(blocks):
        for chunk in range(STEPS // 2):
            at = (block * STEPS + 2 * chunk) * tile_rows
            label = names[chunk, block : block + 1, :]
            hot[:, at : at + LANES] = (source == label).astype(jnp.float32).astype(jnp.bfloat16)

    for block in range(blocks):
        steps = STEPS // 2 + (block < blocks // 2)
        for near in range(0, STA, 2):
            own = [
                [
                    jnp.broadcast_to(own_spec[block, place, near + more : near + more + 1, :], (STA, LANES))
                    for place in range(3 * WIN)
                ]
                for more in range(2)
            ]
            for step in range(steps):
                far_block = (block - 1 - step) % blocks
                far = [far_spec[far_block, place] for place in range(3 * WIN)]
                rows = []
                for more in range(2):
                    sums = [
                        sum(own[more][place] * far[place] for place in range(kind * WIN, (kind + 1) * WIN))
                        for kind in range(3)
                    ]
                    real, imag = sums[0] + sums[1], sums[2] - sums[0] + sums[1]
                    factor = lax.rsqrt(jnp.maximum(real * real + imag * imag, 1.0))
                    rows.append((real * factor, imag * factor))
                real = jnp.concatenate([rows[0][0], rows[1][0]], axis=0).astype(jnp.bfloat16)
                imag = jnp.concatenate([rows[0][1], rows[1][1]], axis=0).astype(jnp.bfloat16)
                at = (block * STEPS + step) * tile_rows + near * STA
                phat[at : at + 2 * STA, :LANES] = real
                phat[at : at + 2 * STA, LANES:] = imag
                back = blocks - 2 - step
                if back < STEPS:
                    at = (far_block * STEPS + back) * tile_rows + near * STA
                    phat[at : at + 2 * STA, :LANES] = real
                    phat[at : at + 2 * STA, LANES:] = -imag
    total[...] = jnp.dot(hot[...], phat[...], preferred_element_type=jnp.float32)
    lead_move.wait()
    for block in range(blocks):
        at = slice(block * VS_DEV, (block + 1) * VS_DEV)
        real, imag = total[at, :LANES], total[at, LANES:]
        for group in range(groups):
            cosine, sine = lead_ref[group : group + 1, :], lead_ref[groups + group : groups + group + 1, :]
            out_ref[block * groups + group] = jnp.concatenate(
                [real * cosine - imag * sine, real * sine + imag * cosine], axis=1
            ).astype(jnp.bfloat16)


def pairs(got, lead):
    blocks, groups = got.shape[0], lead.shape[0] // 2
    sources, rows = blocks * VS_DEV, blocks * STEPS * STA * STA
    return pl.pallas_call(
        pair_kernel,
        out_shape=pltpu.VMEM((blocks * groups, VS_DEV, 2 * LANES), jnp.bfloat16),
        in_specs=[VMEM, pl.BlockSpec(memory_space=pltpu.HBM)],
        out_specs=VMEM,
        compiler_params=pltpu.CompilerParams(vmem_limit_bytes=KERNEL_VMEM),
        scratch_shapes=[
            pltpu.VMEM(lead.shape, lead.dtype),
            pltpu.VMEM((blocks, SPEC_TILES * WIN, LANES), jnp.float32),
            pltpu.VMEM((blocks * WIN, LANES), jnp.float32),
            pltpu.VMEM((blocks, 3 * WIN, STA, LANES), jnp.float32),
            pltpu.VMEM((blocks, 3 * WIN, STA, LANES), jnp.float32),
            pltpu.VMEM((STEPS // 2, blocks, LANES), jnp.float32),
            pltpu.VMEM((rows, 2 * LANES), jnp.bfloat16),
            pltpu.VMEM((sources, rows), jnp.bfloat16),
            pltpu.VMEM((sources, 2 * LANES), jnp.float32),
            pltpu.SemaphoreType.DMA,
        ],
    )(got, pltpu.with_memory_space_constraint(lead, pltpu.HBM))


def lag_kernel(bins_ref, wave_ref, turn_ref, out_ref):
    chunks = bins_ref.shape[0]
    rows = bins_ref[...].reshape(chunks * VS_DEV, 2 * LANES)
    for tile in range(wave_ref.shape[1]):
        lags = jnp.dot(rows, wave_ref[0, tile], preferred_element_type=jnp.float32) + jnp.dot(
            rows, wave_ref[1, tile], preferred_element_type=jnp.float32
        )
        total = jnp.zeros((VS_DEV, LANES), jnp.float32)
        for chunk in range(chunks):
            piece = lags[chunk * VS_DEV : (chunk + 1) * VS_DEV]
            total += piece[:, :LANES] * turn_ref[0, chunk : chunk + 1, :]
            total -= piece[:, LANES:] * turn_ref[1, chunk : chunk + 1, :]
        out_ref[:, tile * LANES : (tile + 1) * LANES] = total


def lags_of(bins, wave, turn):
    return pl.pallas_call(
        lag_kernel,
        out_shape=jax.ShapeDtypeStruct((VS_DEV, wave.shape[1] * LANES), jnp.float32),
        in_specs=[VMEM] * 3,
        out_specs=VMEM,
        compiler_params=pltpu.CompilerParams(vmem_limit_bytes=KERNEL_VMEM),
    )(bins, wave, turn)


def turns(phase):
    angle = np.mod(phase, 2 * BINS) * (math.pi / BINS)
    return np.cos(angle), np.sin(angle)


def lag_tables(blocks, groups):
    lag_dev = LAGS // groups
    first = np.arange(groups) * lag_dev - LAGS // 2
    bins = np.arange(LANES)
    lead = np.concatenate(turns(first[:, None] * bins[None, :])).astype(np.float32)
    cosine, sine = turns(bins[:, None] * np.arange(lag_dev)[None, :])
    tiles = []
    for at in range(0, lag_dev, LANES):
        part = slice(at, at + LANES)
        tiles.append(np.block([[cosine[:, part], sine[:, part]], [-sine[:, part], cosine[:, part]]]))
    wave = np.stack(tiles) / math.sqrt(BINS)
    high = wave.astype(jnp.bfloat16)
    low = (wave - high.astype(np.float64)).astype(jnp.bfloat16)
    place = np.arange(blocks * groups)
    chunk = place % groups * blocks + place // groups
    turn = np.stack(turns(LANES * chunk[:, None] * bins[None, :])).astype(np.float32)
    return jnp.asarray(lead), jnp.asarray(np.stack([high, low])), jnp.asarray(turn)


def by_bins(spectra, quality, pair_mask, owners, local_rows):
    blocks, groups = lax.axis_size("blk"), lax.axis_size("grp")
    lead, wave, turn = lag_tables(blocks, groups)
    sent = pack(spectra, quality, pair_mask, owners, local_rows, blocks)
    got = lax.all_to_all(sent, "blk", split_axis=0, concat_axis=0, tiled=True)
    summed = pairs(got, lead)
    bins = lax.all_to_all(summed, ("blk", "grp"), split_axis=0, concat_axis=0, tiled=True)
    return lags_of(bins, wave, turn)


def from_behind(array, axis, by):
    size = lax.axis_size(axis)
    return lax.ppermute(array, axis, [(i, (i + by) % size) for i in range(size)])


def lag_table(bins_index, total_bins, lags):
    shifts = jnp.arange(lags, dtype=jnp.int32) - lags // 2
    phase = jnp.mod(bins_index[:, None] * shifts[None, :], 2 * total_bins)
    angle = phase.astype(jnp.float32) * (math.pi / total_bins)
    factor = 1.0 / math.sqrt(total_bins)
    return jnp.concatenate([jnp.cos(angle) * factor, -jnp.sin(angle) * factor], axis=0).astype(
        jnp.bfloat16
    )


def phase_rows(own_spec, own_weight, far_spec, far_weight, sub_mask):
    near_weight = own_weight.astype(jnp.float32)[:, :, None]
    away_weight = far_weight.astype(jnp.float32)[:, :, None]
    a_real = own_spec[0].astype(jnp.float32) * near_weight
    a_imag = own_spec[1].astype(jnp.float32) * near_weight
    b_real = far_spec[0].astype(jnp.float32) * away_weight
    b_imag = far_spec[1].astype(jnp.float32) * away_weight
    cross_real = jnp.sum(a_real[:, None] * b_real[None] + a_imag[:, None] * b_imag[None], axis=2)
    cross_imag = jnp.sum(a_imag[:, None] * b_real[None] - a_real[:, None] * b_imag[None], axis=2)
    station_mask = jnp.repeat(jnp.repeat(sub_mask, SUB, axis=0), SUB, axis=1).astype(jnp.float32)
    factor = station_mask[:, :, None] * lax.rsqrt(
        jnp.maximum(cross_real * cross_real + cross_imag * cross_imag, 1.0)
    )
    joined = jnp.concatenate([cross_real * factor, cross_imag * factor], axis=2).astype(
        jnp.bfloat16
    )
    return joined.reshape(STA * STA, joined.shape[2])


def by_halo(spectra, quality, pair_mask, owners, local_rows):
    bins_dev = spectra.shape[3]
    blocks = lax.axis_size("blk")
    rows_dev = owners.shape[0]
    capacity = max(2, 2 * rows_dev // blocks)
    masks = pair_mask[0]
    pieces = [None] * STEPS
    visiting = (spectra, quality)
    for offset in range(STEPS):
        visiting = from_behind((visiting[0], visiting[1]), "blk", 1)
        pieces[offset] = phase_rows(spectra, quality, visiting[0], visiting[1], masks[offset])
    rows_all = jnp.concatenate(pieces, axis=0)
    owner_flat = owners[:, 0]
    row_index = jnp.arange(rows_dev, dtype=jnp.int32)
    earlier = (owner_flat[:, None] == owner_flat[None, :]) & (
        row_index[None, :] < row_index[:, None]
    )
    position = jnp.sum(earlier.astype(jnp.int32), axis=1)
    slot_index = owner_flat * capacity + position
    sources = jnp.arange(VS_DEV, dtype=jnp.int32)
    bins_index = lax.axis_index("grp") * bins_dev + jnp.arange(bins_dev, dtype=jnp.int32)
    table = lag_table(bins_index, BINS, LAGS)
    lag_dev = LAGS // lax.axis_size("grp")
    lag_terms = lax.psum_scatter(
        lax.dot_general(
            table, rows_all, (((0,), (1,)), ((), ())), preferred_element_type=jnp.float32
        ),
        "grp",
        scatter_dimension=0,
        tiled=True,
    )
    outgoing = jnp.zeros((lag_dev, blocks * capacity), jnp.float32).at[:, slot_index].set(lag_terms)
    labels = jnp.full((1, blocks * capacity), -1, jnp.int32).at[0, slot_index].set(local_rows)
    received, got_labels = (
        lax.all_to_all(outgoing, "blk", split_axis=1, concat_axis=1, tiled=True),
        lax.all_to_all(labels, "blk", split_axis=1, concat_axis=1, tiled=True),
    )
    selector = (got_labels == sources[:, None]).astype(jnp.float32)
    stack = lax.dot_general(
        selector,
        received,
        (((1,), (1,)), ((), ())),
        precision=lax.Precision.HIGHEST,
        preferred_element_type=jnp.float32,
    )
    return stack


def on_device(spectra, quality, pair_mask, owners, local_rows):
    blocks, groups = lax.axis_size("blk"), lax.axis_size("grp")
    whole_tiles = spectra.shape[3] == blocks * LANES and LANES * (LAGS // groups) % (2 * BINS) == 0
    if whole_tiles and blocks == STEPS + 2:
        return by_bins(spectra, quality, pair_mask, owners, local_rows)
    return by_halo(spectra, quality, pair_mask, owners, local_rows)


def solution(mesh):
    in_specs = (
        P(None, "blk", None, "grp"),
        P("blk", None),
        P("blk", None, None, None),
        P("blk", None),
        P("blk"),
    )
    out_specs = P("blk", "grp")
    return jax.shard_map(
        on_device, mesh=mesh, in_specs=in_specs, out_specs=out_specs, check_vma=False
    )
```

```python
import functools
import math

import jax
import jax.numpy as jnp
import numpy as np
from jax import lax
from jax.experimental import pallas as pl
from jax.experimental.pallas import tpu as pltpu
from jax.sharding import PartitionSpec as P

STA = 8
WIN = 4
BINS = 4096
LAGS = 2048
STEPS = 6
SUB = 4
VS_DEV = 16
LANES = 128
SPEC_TILES = 2 * STA
KERNEL_VMEM = 12 * 1024 * 1024

VMEM = pl.BlockSpec(memory_space=pltpu.VMEM)


def pack_kernel(spec_hbm, weight_hbm, mask_hbm, owner_hbm, local_hbm, out_ref, weight_ref, mask_ref, owner_ref, local_ref, sliced, arrived):
    dests = out_ref.shape[0]
    slices = [
        pltpu.make_async_copy(
            spec_hbm.at[:, :, pl.ds(dest * LANES, LANES)],
            out_ref.at[dest, pl.ds(0, SPEC_TILES)],
            sliced.at[dest],
        )
        for dest in range(dests)
    ]
    small = [(weight_hbm, weight_ref), (mask_hbm, mask_ref), (owner_hbm, owner_ref), (local_hbm, local_ref)]
    moves = [
        pltpu.make_async_copy(source, target, arrived.at[place])
        for place, (source, target) in enumerate(small)
    ]
    for move in moves + slices:
        move.start()
    lane = lax.broadcasted_iota(jnp.int32, (1, LANES), 1)
    for move in moves:
        move.wait()
    rows = []
    for chunk in range(STEPS // 2):
        part = slice(chunk * LANES, (chunk + 1) * LANES)
        mask = jnp.zeros((1, LANES), jnp.int32)
        for odd in range(2):
            for near in range(2):
                for far in range(2):
                    here = (lane // 64 == odd) & (lane % 64 // 32 == near) & (lane % 8 // 4 == far)
                    step = chunk * 2 + odd
                    mask = jnp.where(here, mask_ref[near, far : far + 1, step : step + 1], mask)
        source = owner_ref[:, part] * VS_DEV + local_ref[part].reshape(1, LANES)
        rows.append(jnp.where(mask != 0, source, -1).astype(jnp.float32))
    weights = [weight_ref[window : window + 1, :].astype(jnp.float32) for window in range(WIN)]
    rows.append(jnp.concatenate(weights + [jnp.zeros((1, LANES - WIN * STA), jnp.float32)], axis=1))
    meta = jnp.concatenate(rows, axis=0).astype(jnp.bfloat16)
    for dest in range(dests):
        out_ref[dest, SPEC_TILES] = meta
    for move in slices:
        move.wait()


def pack(spectra, quality, pair_mask, owners, local_rows, blocks):
    rows = owners.shape[0]
    operands = (
        spectra.reshape(SPEC_TILES, WIN, spectra.shape[3]),
        quality.T,
        pair_mask[0].transpose(1, 2, 0),
        owners.reshape(1, rows),
        local_rows,
    )
    return pl.pallas_call(
        pack_kernel,
        out_shape=pltpu.VMEM((blocks, SPEC_TILES + 1, WIN, LANES), jnp.bfloat16),
        in_specs=[pl.BlockSpec(memory_space=pltpu.HBM)] * len(operands),
        out_specs=VMEM,
        compiler_params=pltpu.CompilerParams(vmem_limit_bytes=KERNEL_VMEM),
        scratch_shapes=[pltpu.VMEM(each.shape, each.dtype) for each in operands[1:]]
        + [pltpu.SemaphoreType.DMA((blocks,)), pltpu.SemaphoreType.DMA((len(operands) - 1,))],
    )(*[pltpu.with_memory_space_constraint(each, pltpu.HBM) for each in operands])


def pair_kernel(got_ref, lead_hbm, out_ref, lead_ref, plain, meta, own_spec, far_spec, names, phat, hot, total, arrived):
    blocks = got_ref.shape[0]
    groups = out_ref.shape[0] // blocks
    sources = blocks * VS_DEV
    tile_rows = STA * STA
    chunk_here = lax.axis_index("grp") * blocks + lax.axis_index("blk")
    lead_move = pltpu.make_async_copy(lead_hbm.at[chunk_here], lead_ref, arrived)
    lead_move.start()

    for block in range(blocks):
        for tile in range(SPEC_TILES):
            plain[block, tile * WIN : (tile + 1) * WIN, :] = got_ref[block, tile].astype(jnp.float32)
        meta[block * WIN : (block + 1) * WIN, :] = got_ref[block, SPEC_TILES].astype(jnp.float32)
    weights = meta[pl.ds(WIN - 1, blocks, stride=WIN), :]
    station_of = lax.broadcasted_iota(jnp.int32, (STA, LANES), 0)
    on_lane = lax.broadcasted_iota(jnp.int32, (STA, LANES), 1)
    for block in range(blocks):
        for window in range(WIN):
            mine = jnp.where(on_lane == window * STA + station_of, weights[block : block + 1, :], 0.0)
            column = jnp.sum(mine, axis=1, keepdims=True)
            real = plain[block, pl.ds(window, STA, stride=WIN), :] * column
            imag = plain[block, pl.ds(STA * WIN + window, STA, stride=WIN), :] * column
            for place, (near, far) in enumerate([(real, real), (imag, imag), (real + imag, real - imag)]):
                own_spec[block, place * WIN + window] = near
                far_spec[block, place * WIN + window] = far

    lane_in = lax.broadcasted_iota(jnp.int32, (LANES, LANES), 0)
    lane_out = lax.broadcasted_iota(jnp.int32, (LANES, LANES), 1)
    turned = lane_out // tile_rows * tile_rows + lane_out % STA * STA + lane_out % tile_rows // STA
    swap = (lane_in == turned).astype(jnp.float32).astype(jnp.bfloat16)
    for chunk in range(STEPS // 2):
        here = meta[pl.ds(chunk, blocks, stride=WIN), :]
        if chunk:
            other = jnp.dot(here.astype(jnp.bfloat16), swap, preferred_element_type=jnp.float32)
            if chunk == 1:
                block_of = lax.broadcasted_iota(jnp.int32, here.shape, 0)
                lane = lax.broadcasted_iota(jnp.int32, here.shape, 1)
                other = jnp.where((block_of >= blocks // 2) & (lane >= tile_rows), other, here)
            here = other
        names[chunk] = here
    source = lax.broadcasted_iota(jnp.int32, (sources, LANES), 0).astype(jnp.float32)
    for block in range(blocks):
        for chunk in range(STEPS // 2):
            at = (block * STEPS + 2 * chunk) * tile_rows
            label = names[chunk, block : block + 1, :]
            hot[:, at : at + LANES] = (source == label).astype(jnp.float32).astype(jnp.bfloat16)

    for block in range(blocks):
        steps = STEPS // 2 + (block < blocks // 2)
        for near in range(0, STA, 2):
            own = [
                [
                    jnp.broadcast_to(own_spec[block, place, near + more : near + more + 1, :], (STA, LANES))
                    for place in range(3 * WIN)
                ]
                for more in range(2)
            ]
            for step in range(steps):
                far_block = (block - 1 - step) % blocks
                far = [far_spec[far_block, place] for place in range(3 * WIN)]
                rows = []
                for more in range(2):
                    sums = [
                        sum(own[more][place] * far[place] for place in range(kind * WIN, (kind + 1) * WIN))
                        for kind in range(3)
                    ]
                    real, imag = sums[0] + sums[1], sums[2] - sums[0] + sums[1]
                    factor = lax.rsqrt(jnp.maximum(real * real + imag * imag, 1.0))
                    rows.append((real * factor, imag * factor))
                real = jnp.concatenate([rows[0][0], rows[1][0]], axis=0).astype(jnp.bfloat16)
                imag = jnp.concatenate([rows[0][1], rows[1][1]], axis=0).astype(jnp.bfloat16)
                at = (block * STEPS + step) * tile_rows + near * STA
                phat[at : at + 2 * STA, :LANES] = real
                phat[at : at + 2 * STA, LANES:] = imag
                back = blocks - 2 - step
                if back < STEPS:
                    at = (far_block * STEPS + back) * tile_rows + near * STA
                    phat[at : at + 2 * STA, :LANES] = real
                    phat[at : at + 2 * STA, LANES:] = -imag
    total[...] = jnp.dot(hot[...], phat[...], preferred_element_type=jnp.float32)
    lead_move.wait()
    for block in range(blocks):
        at = slice(block * VS_DEV, (block + 1) * VS_DEV)
        real, imag = total[at, :LANES], total[at, LANES:]
        for group in range(groups):
            cosine, sine = lead_ref[group : group + 1, :], lead_ref[groups + group : groups + group + 1, :]
            out_ref[block * groups + group] = jnp.concatenate(
                [real * cosine - imag * sine, real * sine + imag * cosine], axis=1
            ).astype(jnp.bfloat16)


def pairs(got, lead):
    blocks, groups = got.shape[0], lead.shape[1] // 2
    sources, rows = blocks * VS_DEV, blocks * STEPS * STA * STA
    return pl.pallas_call(
        pair_kernel,
        out_shape=pltpu.VMEM((blocks * groups, VS_DEV, 2 * LANES), jnp.bfloat16),
        in_specs=[VMEM, pl.BlockSpec(memory_space=pltpu.HBM)],
        out_specs=VMEM,
        compiler_params=pltpu.CompilerParams(vmem_limit_bytes=KERNEL_VMEM),
        scratch_shapes=[
            pltpu.VMEM(lead.shape[1:], lead.dtype),
            pltpu.VMEM((blocks, SPEC_TILES * WIN, LANES), jnp.float32),
            pltpu.VMEM((blocks * WIN, LANES), jnp.float32),
            pltpu.VMEM((blocks, 3 * WIN, STA, LANES), jnp.float32),
            pltpu.VMEM((blocks, 3 * WIN, STA, LANES), jnp.float32),
            pltpu.VMEM((STEPS // 2, blocks, LANES), jnp.float32),
            pltpu.VMEM((rows, 2 * LANES), jnp.bfloat16),
            pltpu.VMEM((sources, rows), jnp.bfloat16),
            pltpu.VMEM((sources, 2 * LANES), jnp.float32),
            pltpu.SemaphoreType.DMA,
        ],
    )(got, pltpu.with_memory_space_constraint(lead, pltpu.HBM))


def lag_kernel(bins_ref, wave_ref, turn_ref, out_ref):
    chunks = bins_ref.shape[0]
    rows = bins_ref[...].reshape(chunks * VS_DEV, 2 * LANES)
    twice = [jnp.concatenate([rows[:, part * LANES : (part + 1) * LANES]] * 2, axis=1) for part in range(2)]
    tiles = wave_ref.shape[0]
    mirror = LANES - 1 - lax.broadcasted_iota(jnp.int32, (VS_DEV, LANES), 1)
    for tile in range(tiles):
        real, imag = [jnp.dot(each, wave_ref[tile], preferred_element_type=jnp.float32) for each in twice]
        even, odd = jnp.zeros((VS_DEV, LANES), jnp.float32), jnp.zeros((VS_DEV, LANES), jnp.float32)
        for chunk in range(chunks):
            at = slice(chunk * VS_DEV, (chunk + 1) * VS_DEV)
            cosine, sine = turn_ref[0, chunk : chunk + 1, :], turn_ref[1, chunk : chunk + 1, :]
            even += real[at, :LANES] * cosine - real[at, LANES:] * sine
            odd += imag[at, :LANES] * sine + imag[at, LANES:] * cosine
        after, before = tiles + tile, tiles - 1 - tile
        out_ref[:, after * LANES : (after + 1) * LANES] = even - odd
        out_ref[:, before * LANES : (before + 1) * LANES] = jnp.take_along_axis(even + odd, mirror, axis=1)


def lags_of(bins, wave, turn):
    return pl.pallas_call(
        lag_kernel,
        out_shape=jax.ShapeDtypeStruct((VS_DEV, 2 * wave.shape[0] * LANES), jnp.float32),
        in_specs=[VMEM] * 3,
        out_specs=VMEM,
        compiler_params=pltpu.CompilerParams(vmem_limit_bytes=KERNEL_VMEM),
    )(bins, wave, turn)


def turns(phase):
    angle = np.mod(phase, 2 * BINS) * (math.pi / BINS)
    return np.cos(angle), np.sin(angle)


def lag_tables(blocks, groups):
    lag_dev = LAGS // groups
    chunks = blocks * groups
    middle = np.arange(groups) * lag_dev - LAGS // 2 + (lag_dev - 1) / 2
    bins = np.arange(LANES)
    whole = LANES * np.arange(chunks)[:, None, None] + bins
    lead = np.concatenate(turns(whole * middle[:, None]), axis=1).astype(np.float32)
    tiles = []
    for first in range(0, lag_dev // 2, LANES):
        tiles.append(np.concatenate(turns(bins[:, None] * (first + bins + 0.5)), axis=1))
    wave = np.stack(tiles) / math.sqrt(BINS)
    high = wave.astype(jnp.bfloat16)
    low = (wave - high.astype(np.float64)).astype(jnp.bfloat16)
    place = np.arange(chunks)
    chunk = place % groups * blocks + place // groups
    turn = np.stack(turns(LANES * chunk[:, None] * (bins + 0.5))).astype(np.float32)
    return jnp.asarray(lead), jnp.asarray(np.concatenate([high, low], axis=1)), jnp.asarray(turn)


def by_bins(spectra, quality, pair_mask, owners, local_rows):
    blocks, groups = lax.axis_size("blk"), lax.axis_size("grp")
    lead, wave, turn = lag_tables(blocks, groups)
    sent = pack(spectra, quality, pair_mask, owners, local_rows, blocks)
    got = lax.all_to_all(sent, "blk", split_axis=0, concat_axis=0, tiled=True)
    summed = pairs(got, lead)
    bins = lax.all_to_all(summed, ("blk", "grp"), split_axis=0, concat_axis=0, tiled=True)
    return lags_of(bins, wave, turn)


def from_behind(array, axis, by):
    size = lax.axis_size(axis)
    return lax.ppermute(array, axis, [(i, (i + by) % size) for i in range(size)])


def lag_table(bins_index, total_bins, lags):
    shifts = jnp.arange(lags, dtype=jnp.int32) - lags // 2
    phase = jnp.mod(bins_index[:, None] * shifts[None, :], 2 * total_bins)
    angle = phase.astype(jnp.float32) * (math.pi / total_bins)
    factor = 1.0 / math.sqrt(total_bins)
    return jnp.concatenate([jnp.cos(angle) * factor, -jnp.sin(angle) * factor], axis=0).astype(
        jnp.bfloat16
    )


def phase_rows(own_spec, own_weight, far_spec, far_weight, sub_mask):
    near_weight = own_weight.astype(jnp.float32)[:, :, None]
    away_weight = far_weight.astype(jnp.float32)[:, :, None]
    a_real = own_spec[0].astype(jnp.float32) * near_weight
    a_imag = own_spec[1].astype(jnp.float32) * near_weight
    b_real = far_spec[0].astype(jnp.float32) * away_weight
    b_imag = far_spec[1].astype(jnp.float32) * away_weight
    cross_real = jnp.sum(a_real[:, None] * b_real[None] + a_imag[:, None] * b_imag[None], axis=2)
    cross_imag = jnp.sum(a_imag[:, None] * b_real[None] - a_real[:, None] * b_imag[None], axis=2)
    station_mask = jnp.repeat(jnp.repeat(sub_mask, SUB, axis=0), SUB, axis=1).astype(jnp.float32)
    factor = station_mask[:, :, None] * lax.rsqrt(
        jnp.maximum(cross_real * cross_real + cross_imag * cross_imag, 1.0)
    )
    joined = jnp.concatenate([cross_real * factor, cross_imag * factor], axis=2).astype(
        jnp.bfloat16
    )
    return joined.reshape(STA * STA, joined.shape[2])


def by_halo(spectra, quality, pair_mask, owners, local_rows):
    bins_dev = spectra.shape[3]
    blocks = lax.axis_size("blk")
    rows_dev = owners.shape[0]
    capacity = max(2, 2 * rows_dev // blocks)
    masks = pair_mask[0]
    pieces = [None] * STEPS
    visiting = (spectra, quality)
    for offset in range(STEPS):
        visiting = from_behind((visiting[0], visiting[1]), "blk", 1)
        pieces[offset] = phase_rows(spectra, quality, visiting[0], visiting[1], masks[offset])
    rows_all = jnp.concatenate(pieces, axis=0)
    owner_flat = owners[:, 0]
    row_index = jnp.arange(rows_dev, dtype=jnp.int32)
    earlier = (owner_flat[:, None] == owner_flat[None, :]) & (
        row_index[None, :] < row_index[:, None]
    )
    position = jnp.sum(earlier.astype(jnp.int32), axis=1)
    slot_index = owner_flat * capacity + position
    sources = jnp.arange(VS_DEV, dtype=jnp.int32)
    bins_index = lax.axis_index("grp") * bins_dev + jnp.arange(bins_dev, dtype=jnp.int32)
    table = lag_table(bins_index, BINS, LAGS)
    lag_dev = LAGS // lax.axis_size("grp")
    lag_terms = lax.psum_scatter(
        lax.dot_general(
            table, rows_all, (((0,), (1,)), ((), ())), preferred_element_type=jnp.float32
        ),
        "grp",
        scatter_dimension=0,
        tiled=True,
    )
    outgoing = jnp.zeros((lag_dev, blocks * capacity), jnp.float32).at[:, slot_index].set(lag_terms)
    labels = jnp.full((1, blocks * capacity), -1, jnp.int32).at[0, slot_index].set(local_rows)
    received, got_labels = (
        lax.all_to_all(outgoing, "blk", split_axis=1, concat_axis=1, tiled=True),
        lax.all_to_all(labels, "blk", split_axis=1, concat_axis=1, tiled=True),
    )
    selector = (got_labels == sources[:, None]).astype(jnp.float32)
    stack = lax.dot_general(
        selector,
        received,
        (((1,), (1,)), ((), ())),
        precision=lax.Precision.HIGHEST,
        preferred_element_type=jnp.float32,
    )
    return stack


def on_device(spectra, quality, pair_mask, owners, local_rows):
    blocks, groups = lax.axis_size("blk"), lax.axis_size("grp")
    whole_tiles = spectra.shape[3] == blocks * LANES and LAGS // groups % (2 * LANES) == 0
    if whole_tiles and blocks == STEPS + 2:
        return by_bins(spectra, quality, pair_mask, owners, local_rows)
    return by_halo(spectra, quality, pair_mask, owners, local_rows)


def solution(mesh):
    in_specs = (
        P(None, "blk", None, "grp"),
        P("blk", None),
        P("blk", None, None, None),
        P("blk", None),
        P("blk"),
    )
    out_specs = P("blk", "grp")
    return jax.shard_map(
        on_device, mesh=mesh, in_specs=in_specs, out_specs=out_specs, check_vma=False
    )
```

```python
import functools
import math

import jax
import jax.numpy as jnp
import numpy as np
from jax import lax
from jax.experimental import pallas as pl
from jax.experimental.pallas import tpu as pltpu
from jax.sharding import PartitionSpec as P

STA = 8
WIN = 4
BINS = 4096
LAGS = 2048
STEPS = 6
SUB = 4
VS_DEV = 16
LANES = 128
SPEC_TILES = 2 * STA
HALF_TILE = 16
KERNEL_VMEM = 12 * 1024 * 1024

VMEM = pl.BlockSpec(memory_space=pltpu.VMEM)


def pack_kernel(spec_hbm, weight_hbm, mask_hbm, owner_hbm, local_hbm, out_ref, weight_ref, mask_ref, owner_ref, local_ref, sliced, arrived):
    dests = out_ref.shape[0]
    slices = [
        pltpu.make_async_copy(
            spec_hbm.at[:, :, pl.ds(dest * LANES, LANES)],
            out_ref.at[dest, pl.ds(0, SPEC_TILES)],
            sliced.at[dest],
        )
        for dest in range(dests)
    ]
    small = [(weight_hbm, weight_ref), (mask_hbm, mask_ref), (owner_hbm, owner_ref), (local_hbm, local_ref)]
    moves = [
        pltpu.make_async_copy(source, target, arrived.at[place])
        for place, (source, target) in enumerate(small)
    ]
    for move in moves + slices:
        move.start()
    lane = lax.broadcasted_iota(jnp.int32, (1, LANES), 1)
    for move in moves:
        move.wait()
    rows = []
    for chunk in range(STEPS // 2):
        part = slice(chunk * LANES, (chunk + 1) * LANES)
        mask = jnp.zeros((1, LANES), jnp.int32)
        for odd in range(2):
            for near in range(2):
                for far in range(2):
                    here = (lane // 64 == odd) & (lane % 64 // 32 == near) & (lane % 8 // 4 == far)
                    step = chunk * 2 + odd
                    mask = jnp.where(here, mask_ref[near, far : far + 1, step : step + 1], mask)
        source = owner_ref[:, part] * VS_DEV + local_ref[part].reshape(1, LANES)
        rows.append(jnp.where(mask != 0, source, -1).astype(jnp.float32))
    weights = [weight_ref[window : window + 1, :].astype(jnp.float32) for window in range(WIN)]
    rows.append(jnp.concatenate(weights + [jnp.zeros((1, LANES - WIN * STA), jnp.float32)], axis=1))
    meta = jnp.concatenate(rows, axis=0).astype(jnp.bfloat16)
    for dest in range(dests):
        out_ref[dest, SPEC_TILES] = meta
    for move in slices:
        move.wait()


def pack(spectra, quality, pair_mask, owners, local_rows, blocks):
    rows = owners.shape[0]
    operands = (
        spectra.reshape(SPEC_TILES, WIN, spectra.shape[3]),
        quality.T,
        pair_mask[0].transpose(1, 2, 0),
        owners.reshape(1, rows),
        local_rows,
    )
    return pl.pallas_call(
        pack_kernel,
        out_shape=pltpu.VMEM((blocks, SPEC_TILES + 1, WIN, LANES), jnp.bfloat16),
        in_specs=[pl.BlockSpec(memory_space=pltpu.HBM)] * len(operands),
        out_specs=VMEM,
        compiler_params=pltpu.CompilerParams(vmem_limit_bytes=KERNEL_VMEM),
        scratch_shapes=[pltpu.VMEM(each.shape, each.dtype) for each in operands[1:]]
        + [pltpu.SemaphoreType.DMA((blocks,)), pltpu.SemaphoreType.DMA((len(operands) - 1,))],
    )(*[pltpu.with_memory_space_constraint(each, pltpu.HBM) for each in operands])


def pair_kernel(got_ref, lead_hbm, out_ref, lead_ref, plain, meta, own_spec, far_spec, names, phat, hot, total, arrived):
    blocks = got_ref.shape[0]
    groups = out_ref.shape[0] // blocks
    sources = blocks * VS_DEV
    tile_rows = STA * STA
    chunk_here = lax.axis_index("grp") * blocks + lax.axis_index("blk")
    lead_move = pltpu.make_async_copy(lead_hbm.at[chunk_here], lead_ref, arrived)
    lead_move.start()

    for block in range(blocks):
        for tile in range(SPEC_TILES):
            plain[block, tile * WIN : (tile + 1) * WIN, :] = got_ref[block, tile].astype(jnp.float32)
        meta[block * WIN : (block + 1) * WIN, :] = got_ref[block, SPEC_TILES].astype(jnp.float32)
    weights = meta[pl.ds(WIN - 1, blocks, stride=WIN), :]
    station_of = lax.broadcasted_iota(jnp.int32, (STA, LANES), 0)
    on_lane = lax.broadcasted_iota(jnp.int32, (STA, LANES), 1)
    for block in range(blocks):
        for window in range(WIN):
            mine = jnp.where(on_lane == window * STA + station_of, weights[block : block + 1, :], 0.0)
            column = jnp.sum(mine, axis=1, keepdims=True)
            real = plain[block, pl.ds(window, STA, stride=WIN), :] * column
            imag = plain[block, pl.ds(STA * WIN + window, STA, stride=WIN), :] * column
            for place, (near, far) in enumerate([(real, real), (imag, imag), (real + imag, real - imag)]):
                own_spec[block, place * WIN + window] = near
                far_spec[block, place * WIN + window] = far

    lane_in = lax.broadcasted_iota(jnp.int32, (LANES, LANES), 0)
    lane_out = lax.broadcasted_iota(jnp.int32, (LANES, LANES), 1)
    turned = lane_out // tile_rows * tile_rows + lane_out % STA * STA + lane_out % tile_rows // STA
    swap = (lane_in == turned).astype(jnp.float32).astype(jnp.bfloat16)
    for chunk in range(STEPS // 2):
        here = meta[pl.ds(chunk, blocks, stride=WIN), :]
        if chunk:
            other = jnp.dot(here.astype(jnp.bfloat16), swap, preferred_element_type=jnp.float32)
            if chunk == 1:
                block_of = lax.broadcasted_iota(jnp.int32, here.shape, 0)
                lane = lax.broadcasted_iota(jnp.int32, here.shape, 1)
                other = jnp.where((block_of >= blocks // 2) & (lane >= tile_rows), other, here)
            here = other
        names[chunk] = here
    source = lax.broadcasted_iota(jnp.int32, (sources, LANES), 0).astype(jnp.float32).astype(jnp.bfloat16)
    one, zero = jnp.ones((HALF_TILE, LANES), jnp.bfloat16), jnp.zeros((HALF_TILE, LANES), jnp.bfloat16)
    for block in range(blocks):
        for chunk in range(STEPS // 2):
            at = (block * STEPS + 2 * chunk) * tile_rows
            label = names[chunk, block : block + 1, :]
            wanted = jnp.broadcast_to(label, (HALF_TILE, LANES)).astype(jnp.bfloat16)
            for first in range(0, sources, HALF_TILE):
                rows = slice(first, first + HALF_TILE)
                hot[rows, at : at + LANES] = jnp.where(source[rows] == wanted, one, zero)

    for block in range(blocks):
        steps = STEPS // 2 + (block < blocks // 2)
        for near in range(0, STA, 2):
            own = [
                [
                    jnp.broadcast_to(own_spec[block, place, near + more : near + more + 1, :], (STA, LANES))
                    for place in range(3 * WIN)
                ]
                for more in range(2)
            ]
            for step in range(steps):
                far_block = (block - 1 - step) % blocks
                far = [far_spec[far_block, place] for place in range(3 * WIN)]
                rows = []
                for more in range(2):
                    sums = [
                        sum(own[more][place] * far[place] for place in range(kind * WIN, (kind + 1) * WIN))
                        for kind in range(3)
                    ]
                    real, imag = sums[0] + sums[1], sums[2] - sums[0] + sums[1]
                    factor = lax.rsqrt(jnp.maximum(real * real + imag * imag, 1.0))
                    rows.append((real * factor, imag * factor))
                real = jnp.concatenate([rows[0][0], rows[1][0]], axis=0).astype(jnp.bfloat16)
                imag = jnp.concatenate([rows[0][1], rows[1][1]], axis=0).astype(jnp.bfloat16)
                at = (block * STEPS + step) * tile_rows + near * STA
                phat[at : at + 2 * STA, :LANES] = real
                phat[at : at + 2 * STA, LANES:] = imag
                back = blocks - 2 - step
                if back < STEPS:
                    at = (far_block * STEPS + back) * tile_rows + near * STA
                    phat[at : at + 2 * STA, :LANES] = real
                    phat[at : at + 2 * STA, LANES:] = -imag
    total[...] = jnp.dot(hot[...], phat[...], preferred_element_type=jnp.float32)
    lead_move.wait()
    for block in range(blocks):
        at = slice(block * VS_DEV, (block + 1) * VS_DEV)
        real, imag = total[at, :LANES], total[at, LANES:]
        for group in range(groups):
            cosine, sine = lead_ref[group : group + 1, :], lead_ref[groups + group : groups + group + 1, :]
            out_ref[block * groups + group] = jnp.concatenate(
                [real * cosine - imag * sine, real * sine + imag * cosine], axis=1
            ).astype(jnp.bfloat16)


def pairs(got, lead):
    blocks, groups = got.shape[0], lead.shape[1] // 2
    sources, rows = blocks * VS_DEV, blocks * STEPS * STA * STA
    return pl.pallas_call(
        pair_kernel,
        out_shape=pltpu.VMEM((blocks * groups, VS_DEV, 2 * LANES), jnp.bfloat16),
        in_specs=[VMEM, pl.BlockSpec(memory_space=pltpu.HBM)],
        out_specs=VMEM,
        compiler_params=pltpu.CompilerParams(vmem_limit_bytes=KERNEL_VMEM),
        scratch_shapes=[
            pltpu.VMEM(lead.shape[1:], lead.dtype),
            pltpu.VMEM((blocks, SPEC_TILES * WIN + STA, LANES), jnp.float32),
            pltpu.VMEM((blocks * WIN + STA, LANES), jnp.float32),
            pltpu.VMEM((blocks, 3 * WIN, STA, LANES), jnp.float32),
            pltpu.VMEM((blocks, 3 * WIN, STA, LANES), jnp.float32),
            pltpu.VMEM((STEPS // 2, blocks, LANES), jnp.float32),
            pltpu.VMEM((rows, 2 * LANES), jnp.bfloat16),
            pltpu.VMEM((sources, rows), jnp.bfloat16),
            pltpu.VMEM((sources, 2 * LANES), jnp.float32),
            pltpu.SemaphoreType.DMA,
        ],
    )(got, pltpu.with_memory_space_constraint(lead, pltpu.HBM))


def lag_kernel(bins_ref, wave_ref, turn_ref, out_ref):
    chunks = bins_ref.shape[0]
    rows = bins_ref[...].reshape(chunks * VS_DEV, 2 * LANES)
    twice = [jnp.concatenate([rows[:, part * LANES : (part + 1) * LANES]] * 2, axis=1) for part in range(2)]
    tiles = wave_ref.shape[0]
    mirror = LANES - 1 - lax.broadcasted_iota(jnp.int32, (VS_DEV, LANES), 1)
    for tile in range(tiles):
        real, imag = [jnp.dot(each, wave_ref[tile], preferred_element_type=jnp.float32) for each in twice]
        even, odd = jnp.zeros((VS_DEV, LANES), jnp.float32), jnp.zeros((VS_DEV, LANES), jnp.float32)
        for chunk in range(chunks):
            at = slice(chunk * VS_DEV, (chunk + 1) * VS_DEV)
            cosine, sine = turn_ref[0, chunk : chunk + 1, :], turn_ref[1, chunk : chunk + 1, :]
            even += real[at, :LANES] * cosine - real[at, LANES:] * sine
            odd += imag[at, :LANES] * sine + imag[at, LANES:] * cosine
        after, before = tiles + tile, tiles - 1 - tile
        out_ref[:, after * LANES : (after + 1) * LANES] = even - odd
        out_ref[:, before * LANES : (before + 1) * LANES] = jnp.take_along_axis(even + odd, mirror, axis=1)


def lags_of(bins, wave, turn):
    return pl.pallas_call(
        lag_kernel,
        out_shape=jax.ShapeDtypeStruct((VS_DEV, 2 * wave.shape[0] * LANES), jnp.float32),
        in_specs=[VMEM] * 3,
        out_specs=VMEM,
        compiler_params=pltpu.CompilerParams(vmem_limit_bytes=KERNEL_VMEM),
    )(bins, wave, turn)


def turns(phase):
    angle = np.mod(phase, 2 * BINS) * (math.pi / BINS)
    return np.cos(angle), np.sin(angle)


def lag_tables(blocks, groups):
    lag_dev = LAGS // groups
    chunks = blocks * groups
    middle = np.arange(groups) * lag_dev - LAGS // 2 + (lag_dev - 1) / 2
    bins = np.arange(LANES)
    whole = LANES * np.arange(chunks)[:, None, None] + bins
    lead = np.concatenate(turns(whole * middle[:, None]), axis=1).astype(np.float32)
    tiles = []
    for first in range(0, lag_dev // 2, LANES):
        tiles.append(np.concatenate(turns(bins[:, None] * (first + bins + 0.5)), axis=1))
    wave = np.stack(tiles) / math.sqrt(BINS)
    high = wave.astype(jnp.bfloat16)
    low = (wave - high.astype(np.float64)).astype(jnp.bfloat16)
    place = np.arange(chunks)
    chunk = place % groups * blocks + place // groups
    turn = np.stack(turns(LANES * chunk[:, None] * (bins + 0.5))).astype(np.float32)
    return jnp.asarray(lead), jnp.asarray(np.concatenate([high, low], axis=1)), jnp.asarray(turn)


def by_bins(spectra, quality, pair_mask, owners, local_rows):
    blocks, groups = lax.axis_size("blk"), lax.axis_size("grp")
    lead, wave, turn = lag_tables(blocks, groups)
    sent = pack(spectra, quality, pair_mask, owners, local_rows, blocks)
    got = lax.all_to_all(sent, "blk", split_axis=0, concat_axis=0, tiled=True)
    summed = pairs(got, lead)
    bins = lax.all_to_all(summed, ("blk", "grp"), split_axis=0, concat_axis=0, tiled=True)
    return lags_of(bins, wave, turn)


def from_behind(array, axis, by):
    size = lax.axis_size(axis)
    return lax.ppermute(array, axis, [(i, (i + by) % size) for i in range(size)])


def lag_table(bins_index, total_bins, lags):
    shifts = jnp.arange(lags, dtype=jnp.int32) - lags // 2
    phase = jnp.mod(bins_index[:, None] * shifts[None, :], 2 * total_bins)
    angle = phase.astype(jnp.float32) * (math.pi / total_bins)
    factor = 1.0 / math.sqrt(total_bins)
    return jnp.concatenate([jnp.cos(angle) * factor, -jnp.sin(angle) * factor], axis=0).astype(
        jnp.bfloat16
    )


def phase_rows(own_spec, own_weight, far_spec, far_weight, sub_mask):
    near_weight = own_weight.astype(jnp.float32)[:, :, None]
    away_weight = far_weight.astype(jnp.float32)[:, :, None]
    a_real = own_spec[0].astype(jnp.float32) * near_weight
    a_imag = own_spec[1].astype(jnp.float32) * near_weight
    b_real = far_spec[0].astype(jnp.float32) * away_weight
    b_imag = far_spec[1].astype(jnp.float32) * away_weight
    cross_real = jnp.sum(a_real[:, None] * b_real[None] + a_imag[:, None] * b_imag[None], axis=2)
    cross_imag = jnp.sum(a_imag[:, None] * b_real[None] - a_real[:, None] * b_imag[None], axis=2)
    station_mask = jnp.repeat(jnp.repeat(sub_mask, SUB, axis=0), SUB, axis=1).astype(jnp.float32)
    factor = station_mask[:, :, None] * lax.rsqrt(
        jnp.maximum(cross_real * cross_real + cross_imag * cross_imag, 1.0)
    )
    joined = jnp.concatenate([cross_real * factor, cross_imag * factor], axis=2).astype(
        jnp.bfloat16
    )
    return joined.reshape(STA * STA, joined.shape[2])


def by_halo(spectra, quality, pair_mask, owners, local_rows):
    bins_dev = spectra.shape[3]
    blocks = lax.axis_size("blk")
    rows_dev = owners.shape[0]
    capacity = max(2, 2 * rows_dev // blocks)
    masks = pair_mask[0]
    pieces = [None] * STEPS
    visiting = (spectra, quality)
    for offset in range(STEPS):
        visiting = from_behind((visiting[0], visiting[1]), "blk", 1)
        pieces[offset] = phase_rows(spectra, quality, visiting[0], visiting[1], masks[offset])
    rows_all = jnp.concatenate(pieces, axis=0)
    owner_flat = owners[:, 0]
    row_index = jnp.arange(rows_dev, dtype=jnp.int32)
    earlier = (owner_flat[:, None] == owner_flat[None, :]) & (
        row_index[None, :] < row_index[:, None]
    )
    position = jnp.sum(earlier.astype(jnp.int32), axis=1)
    slot_index = owner_flat * capacity + position
    sources = jnp.arange(VS_DEV, dtype=jnp.int32)
    bins_index = lax.axis_index("grp") * bins_dev + jnp.arange(bins_dev, dtype=jnp.int32)
    table = lag_table(bins_index, BINS, LAGS)
    lag_dev = LAGS // lax.axis_size("grp")
    lag_terms = lax.psum_scatter(
        lax.dot_general(
            table, rows_all, (((0,), (1,)), ((), ())), preferred_element_type=jnp.float32
        ),
        "grp",
        scatter_dimension=0,
        tiled=True,
    )
    outgoing = jnp.zeros((lag_dev, blocks * capacity), jnp.float32).at[:, slot_index].set(lag_terms)
    labels = jnp.full((1, blocks * capacity), -1, jnp.int32).at[0, slot_index].set(local_rows)
    received, got_labels = (
        lax.all_to_all(outgoing, "blk", split_axis=1, concat_axis=1, tiled=True),
        lax.all_to_all(labels, "blk", split_axis=1, concat_axis=1, tiled=True),
    )
    selector = (got_labels == sources[:, None]).astype(jnp.float32)
    stack = lax.dot_general(
        selector,
        received,
        (((1,), (1,)), ((), ())),
        precision=lax.Precision.HIGHEST,
        preferred_element_type=jnp.float32,
    )
    return stack


def on_device(spectra, quality, pair_mask, owners, local_rows):
    blocks, groups = lax.axis_size("blk"), lax.axis_size("grp")
    whole_tiles = spectra.shape[3] == blocks * LANES and LAGS // groups % (2 * LANES) == 0
    if whole_tiles and blocks == STEPS + 2:
        return by_bins(spectra, quality, pair_mask, owners, local_rows)
    return by_halo(spectra, quality, pair_mask, owners, local_rows)


def solution(mesh):
    in_specs = (
        P(None, "blk", None, "grp"),
        P("blk", None),
        P("blk", None, None, None),
        P("blk", None),
        P("blk"),
    )
    out_specs = P("blk", "grp")
    return jax.shard_map(
        on_device, mesh=mesh, in_specs=in_specs, out_specs=out_specs, check_vma=False
    )
```

```python
import math

import jax
import jax.numpy as jnp
import numpy as np
from jax import lax
from jax.experimental import pallas as pl
from jax.experimental.pallas import tpu as pltpu
from jax.sharding import PartitionSpec as P

STA = 8
WIN = 4
BINS = 4096
LAGS = 2048
STEPS = 6
SUB = 4
VS_DEV = 16
LANES = 128
SPEC_TILES = 2 * STA
HALF_TILE = 16
KERNEL_VMEM = 12 * 1024 * 1024

VMEM = pl.BlockSpec(memory_space=pltpu.VMEM)


def pack_kernel(spec_hbm, weight_hbm, mask_hbm, owner_hbm, local_hbm, out_ref, weight_ref, mask_ref, owner_ref, local_ref, sliced, arrived):
    dests = out_ref.shape[0]
    slices = [
        pltpu.make_async_copy(
            spec_hbm.at[:, :, pl.ds(dest * LANES, LANES)],
            out_ref.at[dest, pl.ds(0, SPEC_TILES)],
            sliced.at[dest],
        )
        for dest in range(dests)
    ]
    small = [(weight_hbm, weight_ref), (mask_hbm, mask_ref), (owner_hbm, owner_ref), (local_hbm, local_ref)]
    moves = [
        pltpu.make_async_copy(source, target, arrived.at[place])
        for place, (source, target) in enumerate(small)
    ]
    for move in moves + slices:
        move.start()
    lane = lax.broadcasted_iota(jnp.int32, (1, LANES), 1)
    for move in moves:
        move.wait()
    rows = []
    for chunk in range(STEPS // 2):
        part = slice(chunk * LANES, (chunk + 1) * LANES)
        mask = jnp.zeros((1, LANES), jnp.int32)
        for odd in range(2):
            for near in range(2):
                for far in range(2):
                    here = (lane // 64 == odd) & (lane % 64 // 32 == near) & (lane % 8 // 4 == far)
                    step = chunk * 2 + odd
                    mask = jnp.where(here, mask_ref[near, far : far + 1, step : step + 1], mask)
        source = owner_ref[:, part] * VS_DEV + local_ref[part].reshape(1, LANES)
        rows.append(jnp.where(mask != 0, source, -1).astype(jnp.float32))
    weights = [weight_ref[window : window + 1, :].astype(jnp.float32) for window in range(WIN)]
    rows.append(jnp.concatenate(weights + [jnp.zeros((1, LANES - WIN * STA), jnp.float32)], axis=1))
    meta = jnp.concatenate(rows, axis=0).astype(jnp.bfloat16)
    for dest in range(dests):
        out_ref[dest, SPEC_TILES] = meta
    for move in slices:
        move.wait()


def pack(spectra, quality, pair_mask, owners, local_rows, blocks):
    rows = owners.shape[0]
    operands = (
        spectra.reshape(SPEC_TILES, WIN, spectra.shape[3]),
        quality.T,
        pair_mask[0].transpose(1, 2, 0),
        owners.reshape(1, rows),
        local_rows,
    )
    return pl.pallas_call(
        pack_kernel,
        out_shape=pltpu.VMEM((blocks, SPEC_TILES + 1, WIN, LANES), jnp.bfloat16),
        in_specs=[pl.BlockSpec(memory_space=pltpu.HBM)] * len(operands),
        out_specs=VMEM,
        compiler_params=pltpu.CompilerParams(vmem_limit_bytes=KERNEL_VMEM),
        scratch_shapes=[pltpu.VMEM(each.shape, each.dtype) for each in operands[1:]]
        + [pltpu.SemaphoreType.DMA((blocks,)), pltpu.SemaphoreType.DMA((len(operands) - 1,))],
    )(*[pltpu.with_memory_space_constraint(each, pltpu.HBM) for each in operands])


def pair_kernel(got_ref, lead_hbm, out_ref, lead_ref, plain, meta, own_spec, far_spec, names, phat, hot, total, arrived):
    blocks = got_ref.shape[0]
    groups = out_ref.shape[0] // blocks
    sources = blocks * VS_DEV
    tile_rows = STA * STA
    chunk_here = lax.axis_index("grp") * blocks + lax.axis_index("blk")
    lead_move = pltpu.make_async_copy(lead_hbm.at[chunk_here], lead_ref, arrived)
    lead_move.start()

    for block in range(blocks):
        for tile in range(SPEC_TILES):
            plain[block, tile * WIN : (tile + 1) * WIN, :] = got_ref[block, tile].astype(jnp.float32)
        meta[block * WIN : (block + 1) * WIN, :] = got_ref[block, SPEC_TILES].astype(jnp.float32)
    weights = meta[pl.ds(WIN - 1, blocks, stride=WIN), :]
    station_of = lax.broadcasted_iota(jnp.int32, (STA, LANES), 0)
    on_lane = lax.broadcasted_iota(jnp.int32, (STA, LANES), 1)
    for block in range(blocks):
        for window in range(WIN):
            mine = jnp.where(on_lane == window * STA + station_of, weights[block : block + 1, :], 0.0)
            column = jnp.sum(mine, axis=1, keepdims=True)
            real = plain[block, pl.ds(window, STA, stride=WIN), :] * column
            imag = plain[block, pl.ds(STA * WIN + window, STA, stride=WIN), :] * column
            for place, (near, far) in enumerate([(real, real), (imag, imag), (real + imag, real - imag)]):
                own_spec[block, place * WIN + window] = near
                far_spec[block, place * WIN + window] = far

    lane_in = lax.broadcasted_iota(jnp.int32, (LANES, LANES), 0)
    lane_out = lax.broadcasted_iota(jnp.int32, (LANES, LANES), 1)
    turned = lane_out // tile_rows * tile_rows + lane_out % STA * STA + lane_out % tile_rows // STA
    swap = (lane_in == turned).astype(jnp.float32).astype(jnp.bfloat16)
    labels = [meta[pl.ds(chunk, blocks, stride=WIN), :] for chunk in range(STEPS // 2)]
    turned_labels = [
        jnp.dot(each.astype(jnp.bfloat16), swap, preferred_element_type=jnp.float32) for each in labels[1:]
    ]
    names[0], names[1] = labels[0], labels[1]
    names[2], names[3] = turned_labels[1], turned_labels[0]
    names[4], names[5] = pltpu.roll(labels[1], tile_rows, 1), pltpu.roll(turned_labels[1], tile_rows, 1)

    def name(kind, block):
        return names[kind, block % blocks : block % blocks + 1, :]

    source = lax.broadcasted_iota(jnp.int32, (sources, LANES), 0).astype(jnp.float32).astype(jnp.bfloat16)
    one, zero = jnp.ones((HALF_TILE, LANES), jnp.bfloat16), jnp.zeros((HALF_TILE, LANES), jnp.bfloat16)
    low = lax.broadcasted_iota(jnp.int32, (1, LANES), 1) < tile_rows
    half = blocks // 2
    pairs_of = [(name(0, block), jnp.where(low, -1.0, name(2, block - 2))) for block in range(blocks)]
    pairs_of += [(name(1, block), jnp.where(low, name(2, block - 3), name(3, block + half))) for block in range(half)]
    pairs_of += [
        (
            jnp.where(low, name(1, block), name(4, block + 1)),
            jnp.where(low, name(2, block - 3), name(5, block - 2)),
        )
        for block in range(half, blocks, 2)
    ]
    for chunk, both in enumerate(pairs_of):
        at = slice(chunk * LANES, (chunk + 1) * LANES)
        forth, back = [jnp.broadcast_to(each, (HALF_TILE, LANES)).astype(jnp.bfloat16) for each in both]
        for first in range(0, sources, HALF_TILE):
            here = source[first : first + HALF_TILE]
            own_rows, far_rows = jnp.where(here == forth, one, zero), jnp.where(here == back, one, zero)
            hot[first : first + HALF_TILE, at] = own_rows + far_rows
            hot[sources + first : sources + first + HALF_TILE, at] = own_rows - far_rows

    def row_of(block, step):
        if step < 2:
            return block * LANES + step * tile_rows
        if block < half:
            return (blocks + block) * LANES + (step - 2) * tile_rows
        return (blocks + half) * LANES + (block - half) * tile_rows

    for block in range(blocks):
        steps = STEPS // 2 + (block < blocks // 2)
        for near in range(0, STA, 2):
            own = [
                [
                    jnp.broadcast_to(own_spec[block, place, near + more : near + more + 1, :], (STA, LANES))
                    for place in range(3 * WIN)
                ]
                for more in range(2)
            ]
            for step in range(steps):
                far_block = (block - 1 - step) % blocks
                far = [far_spec[far_block, place] for place in range(3 * WIN)]
                rows = []
                for more in range(2):
                    sums = [
                        sum(own[more][place] * far[place] for place in range(kind * WIN, (kind + 1) * WIN))
                        for kind in range(3)
                    ]
                    real, imag = sums[0] + sums[1], sums[2] - sums[0] + sums[1]
                    factor = lax.rsqrt(jnp.maximum(real * real + imag * imag, 1.0))
                    rows.append((real * factor, imag * factor))
                real = jnp.concatenate([rows[0][0], rows[1][0]], axis=0).astype(jnp.bfloat16)
                imag = jnp.concatenate([rows[0][1], rows[1][1]], axis=0).astype(jnp.bfloat16)
                at = row_of(block, step) + near * STA
                phat[at : at + 2 * STA, :LANES] = real
                phat[at : at + 2 * STA, LANES:] = imag
    total[...] = jnp.dot(hot[...], phat[...], preferred_element_type=jnp.float32)
    lead_move.wait()
    for block in range(blocks):
        at = slice(block * VS_DEV, (block + 1) * VS_DEV)
        real, imag = total[at, :LANES], total[sources + block * VS_DEV : sources + (block + 1) * VS_DEV, LANES:]
        for group in range(groups):
            cosine, sine = lead_ref[group : group + 1, :], lead_ref[groups + group : groups + group + 1, :]
            out_ref[block * groups + group] = jnp.concatenate(
                [real * cosine - imag * sine, real * sine + imag * cosine], axis=1
            ).astype(jnp.bfloat16)


def pairs(got, lead):
    blocks, groups = got.shape[0], lead.shape[1] // 2
    sources, rows = blocks * VS_DEV, blocks * STEPS * STA * STA * 7 // 12
    return pl.pallas_call(
        pair_kernel,
        out_shape=pltpu.VMEM((blocks * groups, VS_DEV, 2 * LANES), jnp.bfloat16),
        in_specs=[VMEM, pl.BlockSpec(memory_space=pltpu.HBM)],
        out_specs=VMEM,
        compiler_params=pltpu.CompilerParams(vmem_limit_bytes=KERNEL_VMEM),
        scratch_shapes=[
            pltpu.VMEM(lead.shape[1:], lead.dtype),
            pltpu.VMEM((blocks, SPEC_TILES * WIN + STA, LANES), jnp.float32),
            pltpu.VMEM((blocks * WIN + STA, LANES), jnp.float32),
            pltpu.VMEM((blocks, 3 * WIN, STA, LANES), jnp.float32),
            pltpu.VMEM((blocks, 3 * WIN, STA, LANES), jnp.float32),
            pltpu.VMEM((STEPS, blocks, LANES), jnp.float32),
            pltpu.VMEM((rows, 2 * LANES), jnp.bfloat16),
            pltpu.VMEM((2 * sources, rows), jnp.bfloat16),
            pltpu.VMEM((2 * sources, 2 * LANES), jnp.float32),
            pltpu.SemaphoreType.DMA,
        ],
    )(got, pltpu.with_memory_space_constraint(lead, pltpu.HBM))


def lag_kernel(bins_ref, wave_ref, turn_ref, out_ref):
    chunks = bins_ref.shape[0]
    rows = bins_ref[...].reshape(chunks * VS_DEV, 2 * LANES)
    twice = [jnp.concatenate([rows[:, part * LANES : (part + 1) * LANES]] * 2, axis=1) for part in range(2)]
    tiles = wave_ref.shape[0]
    mirror = LANES - 1 - lax.broadcasted_iota(jnp.int32, (VS_DEV, LANES), 1)
    for tile in range(tiles):
        real, imag = [jnp.dot(each, wave_ref[tile], preferred_element_type=jnp.float32) for each in twice]
        even, odd = jnp.zeros((VS_DEV, LANES), jnp.float32), jnp.zeros((VS_DEV, LANES), jnp.float32)
        for chunk in range(chunks):
            at = slice(chunk * VS_DEV, (chunk + 1) * VS_DEV)
            cosine, sine = turn_ref[0, chunk : chunk + 1, :], turn_ref[1, chunk : chunk + 1, :]
            even += real[at, :LANES] * cosine - real[at, LANES:] * sine
            odd += imag[at, :LANES] * sine + imag[at, LANES:] * cosine
        after, before = tiles + tile, tiles - 1 - tile
        out_ref[:, after * LANES : (after + 1) * LANES] = even - odd
        out_ref[:, before * LANES : (before + 1) * LANES] = jnp.take_along_axis(even + odd, mirror, axis=1)


def lags_of(bins, wave, turn):
    return pl.pallas_call(
        lag_kernel,
        out_shape=jax.ShapeDtypeStruct((VS_DEV, 2 * wave.shape[0] * LANES), jnp.float32),
        in_specs=[VMEM] * 3,
        out_specs=VMEM,
        compiler_params=pltpu.CompilerParams(vmem_limit_bytes=KERNEL_VMEM),
    )(bins, wave, turn)


def turns(phase):
    angle = np.mod(phase, 2 * BINS) * (math.pi / BINS)
    return np.cos(angle), np.sin(angle)


def lag_tables(blocks, groups):
    lag_dev = LAGS // groups
    chunks = blocks * groups
    middle = np.arange(groups) * lag_dev - LAGS // 2 + (lag_dev - 1) / 2
    bins = np.arange(LANES)
    whole = LANES * np.arange(chunks)[:, None, None] + bins
    lead = np.concatenate(turns(whole * middle[:, None]), axis=1).astype(np.float32)
    tiles = []
    for first in range(0, lag_dev // 2, LANES):
        tiles.append(np.concatenate(turns(bins[:, None] * (first + bins + 0.5)), axis=1))
    wave = np.stack(tiles) / math.sqrt(BINS)
    high = wave.astype(jnp.bfloat16)
    low = (wave - high.astype(np.float64)).astype(jnp.bfloat16)
    place = np.arange(chunks)
    chunk = place % groups * blocks + place // groups
    turn = np.stack(turns(LANES * chunk[:, None] * (bins + 0.5))).astype(np.float32)
    return jnp.asarray(lead), jnp.asarray(np.concatenate([high, low], axis=1)), jnp.asarray(turn)


def by_bins(spectra, quality, pair_mask, owners, local_rows):
    blocks, groups = lax.axis_size("blk"), lax.axis_size("grp")
    lead, wave, turn = lag_tables(blocks, groups)
    sent = pack(spectra, quality, pair_mask, owners, local_rows, blocks)
    got = lax.all_to_all(sent, "blk", split_axis=0, concat_axis=0, tiled=True)
    summed = pairs(got, lead)
    bins = lax.all_to_all(summed, ("blk", "grp"), split_axis=0, concat_axis=0, tiled=True)
    return lags_of(bins, wave, turn)


def from_behind(array, axis, by):
    size = lax.axis_size(axis)
    return lax.ppermute(array, axis, [(i, (i + by) % size) for i in range(size)])


def lag_table(bins_index, total_bins, lags):
    shifts = jnp.arange(lags, dtype=jnp.int32) - lags // 2
    phase = jnp.mod(bins_index[:, None] * shifts[None, :], 2 * total_bins)
    angle = phase.astype(jnp.float32) * (math.pi / total_bins)
    factor = 1.0 / math.sqrt(total_bins)
    return jnp.concatenate([jnp.cos(angle) * factor, -jnp.sin(angle) * factor], axis=0).astype(
        jnp.bfloat16
    )


def phase_rows(own_spec, own_weight, far_spec, far_weight, sub_mask):
    near_weight = own_weight.astype(jnp.float32)[:, :, None]
    away_weight = far_weight.astype(jnp.float32)[:, :, None]
    a_real = own_spec[0].astype(jnp.float32) * near_weight
    a_imag = own_spec[1].astype(jnp.float32) * near_weight
    b_real = far_spec[0].astype(jnp.float32) * away_weight
    b_imag = far_spec[1].astype(jnp.float32) * away_weight
    cross_real = jnp.sum(a_real[:, None] * b_real[None] + a_imag[:, None] * b_imag[None], axis=2)
    cross_imag = jnp.sum(a_imag[:, None] * b_real[None] - a_real[:, None] * b_imag[None], axis=2)
    station_mask = jnp.repeat(jnp.repeat(sub_mask, SUB, axis=0), SUB, axis=1).astype(jnp.float32)
    factor = station_mask[:, :, None] * lax.rsqrt(
        jnp.maximum(cross_real * cross_real + cross_imag * cross_imag, 1.0)
    )
    joined = jnp.concatenate([cross_real * factor, cross_imag * factor], axis=2).astype(
        jnp.bfloat16
    )
    return joined.reshape(STA * STA, joined.shape[2])


def by_halo(spectra, quality, pair_mask, owners, local_rows):
    bins_dev = spectra.shape[3]
    blocks = lax.axis_size("blk")
    rows_dev = owners.shape[0]
    capacity = max(2, 2 * rows_dev // blocks)
    masks = pair_mask[0]
    pieces = [None] * STEPS
    visiting = (spectra, quality)
    for offset in range(STEPS):
        visiting = from_behind((visiting[0], visiting[1]), "blk", 1)
        pieces[offset] = phase_rows(spectra, quality, visiting[0], visiting[1], masks[offset])
    rows_all = jnp.concatenate(pieces, axis=0)
    owner_flat = owners[:, 0]
    row_index = jnp.arange(rows_dev, dtype=jnp.int32)
    earlier = (owner_flat[:, None] == owner_flat[None, :]) & (
        row_index[None, :] < row_index[:, None]
    )
    position = jnp.sum(earlier.astype(jnp.int32), axis=1)
    slot_index = owner_flat * capacity + position
    sources = jnp.arange(VS_DEV, dtype=jnp.int32)
    bins_index = lax.axis_index("grp") * bins_dev + jnp.arange(bins_dev, dtype=jnp.int32)
    table = lag_table(bins_index, BINS, LAGS)
    lag_dev = LAGS // lax.axis_size("grp")
    lag_terms = lax.psum_scatter(
        lax.dot_general(
            table, rows_all, (((0,), (1,)), ((), ())), preferred_element_type=jnp.float32
        ),
        "grp",
        scatter_dimension=0,
        tiled=True,
    )
    outgoing = jnp.zeros((lag_dev, blocks * capacity), jnp.float32).at[:, slot_index].set(lag_terms)
    labels = jnp.full((1, blocks * capacity), -1, jnp.int32).at[0, slot_index].set(local_rows)
    received, got_labels = (
        lax.all_to_all(outgoing, "blk", split_axis=1, concat_axis=1, tiled=True),
        lax.all_to_all(labels, "blk", split_axis=1, concat_axis=1, tiled=True),
    )
    selector = (got_labels == sources[:, None]).astype(jnp.float32)
    stack = lax.dot_general(
        selector,
        received,
        (((1,), (1,)), ((), ())),
        precision=lax.Precision.HIGHEST,
        preferred_element_type=jnp.float32,
    )
    return stack


def on_device(spectra, quality, pair_mask, owners, local_rows):
    blocks, groups = lax.axis_size("blk"), lax.axis_size("grp")
    whole_tiles = spectra.shape[3] == blocks * LANES and LAGS // groups % (2 * LANES) == 0
    if whole_tiles and blocks == STEPS + 2:
        return by_bins(spectra, quality, pair_mask, owners, local_rows)
    return by_halo(spectra, quality, pair_mask, owners, local_rows)


def solution(mesh):
    in_specs = (
        P(None, "blk", None, "grp"),
        P("blk", None),
        P("blk", None, None, None),
        P("blk", None),
        P("blk"),
    )
    out_specs = P("blk", "grp")
    return jax.shard_map(
        on_device, mesh=mesh, in_specs=in_specs, out_specs=out_specs, check_vma=False
    )
```

```python
import math

import jax
import jax.numpy as jnp
import numpy as np
from jax import lax
from jax.experimental import pallas as pl
from jax.experimental.pallas import tpu as pltpu
from jax.sharding import PartitionSpec as P

STA = 8
WIN = 4
BINS = 4096
LAGS = 2048
STEPS = 6
SUB = 4
VS_DEV = 16
LANES = 128
SPEC_TILES = 2 * STA
HALF_TILE = 16
KERNEL_VMEM = 12 * 1024 * 1024

VMEM = pl.BlockSpec(memory_space=pltpu.VMEM)


def pack_kernel(spec_hbm, weight_hbm, mask_hbm, owner_hbm, local_hbm, out_ref, weight_ref, mask_ref, owner_ref, local_ref, sliced, arrived):
    dests = out_ref.shape[0]
    slices = [
        pltpu.make_async_copy(
            spec_hbm.at[:, :, pl.ds(dest * LANES, LANES)],
            out_ref.at[dest, pl.ds(0, SPEC_TILES)],
            sliced.at[dest],
        )
        for dest in range(dests)
    ]
    small = [(weight_hbm, weight_ref), (mask_hbm, mask_ref), (owner_hbm, owner_ref), (local_hbm, local_ref)]
    moves = [
        pltpu.make_async_copy(source, target, arrived.at[place])
        for place, (source, target) in enumerate(small)
    ]
    for move in moves + slices:
        move.start()
    lane = lax.broadcasted_iota(jnp.int32, (1, LANES), 1)
    for move in moves:
        move.wait()
    rows = []
    for chunk in range(STEPS // 2):
        part = slice(chunk * LANES, (chunk + 1) * LANES)
        mask = jnp.zeros((1, LANES), jnp.int32)
        for odd in range(2):
            for near in range(2):
                for far in range(2):
                    here = (lane // 64 == odd) & (lane % 64 // 32 == near) & (lane % 8 // 4 == far)
                    step = chunk * 2 + odd
                    mask = jnp.where(here, mask_ref[near, far : far + 1, step : step + 1], mask)
        source = owner_ref[:, part] * VS_DEV + local_ref[part].reshape(1, LANES)
        rows.append(jnp.where(mask != 0, source, -1).astype(jnp.float32))
    weights = [weight_ref[window : window + 1, :].astype(jnp.float32) for window in range(WIN)]
    rows.append(jnp.concatenate(weights + [jnp.zeros((1, LANES - WIN * STA), jnp.float32)], axis=1))
    meta = jnp.concatenate(rows, axis=0).astype(jnp.bfloat16)
    for dest in range(dests):
        out_ref[dest, SPEC_TILES] = meta
    for move in slices:
        move.wait()


def pack(spectra, quality, pair_mask, owners, local_rows, blocks):
    rows = owners.shape[0]
    operands = (
        spectra.reshape(SPEC_TILES, WIN, spectra.shape[3]),
        quality.T,
        pair_mask[0].transpose(1, 2, 0),
        owners.reshape(1, rows),
        local_rows,
    )
    return pl.pallas_call(
        pack_kernel,
        out_shape=pltpu.VMEM((blocks, SPEC_TILES + 1, WIN, LANES), jnp.bfloat16),
        in_specs=[pl.BlockSpec(memory_space=pltpu.HBM)] * len(operands),
        out_specs=VMEM,
        compiler_params=pltpu.CompilerParams(vmem_limit_bytes=KERNEL_VMEM),
        scratch_shapes=[pltpu.VMEM(each.shape, each.dtype) for each in operands[1:]]
        + [pltpu.SemaphoreType.DMA((blocks,)), pltpu.SemaphoreType.DMA((len(operands) - 1,))],
    )(*[pltpu.with_memory_space_constraint(each, pltpu.HBM) for each in operands])


def pair_kernel(got_ref, lead_hbm, out_ref, lead_ref, plain, meta, own_spec, far_spec, names, phat, hot, total, arrived):
    blocks = got_ref.shape[0]
    groups = out_ref.shape[0] // blocks
    sources = blocks * VS_DEV
    tile_rows = STA * STA
    chunk_here = lax.axis_index("grp") * blocks + lax.axis_index("blk")
    lead_move = pltpu.make_async_copy(lead_hbm.at[chunk_here], lead_ref, arrived)
    lead_move.start()

    for block in range(blocks):
        for tile in range(SPEC_TILES):
            plain[block, tile * WIN : (tile + 1) * WIN, :] = got_ref[block, tile].astype(jnp.float32)
        meta[block * WIN : (block + 1) * WIN, :] = got_ref[block, SPEC_TILES].astype(jnp.float32)
    weights = meta[pl.ds(WIN - 1, blocks, stride=WIN), :]
    station_of = lax.broadcasted_iota(jnp.int32, (STA, LANES), 0)
    on_lane = lax.broadcasted_iota(jnp.int32, (STA, LANES), 1)
    for block in range(blocks):
        for window in range(WIN):
            mine = jnp.where(on_lane == window * STA + station_of, weights[block : block + 1, :], 0.0)
            column = jnp.sum(mine, axis=1, keepdims=True)
            real = plain[block, pl.ds(window, STA, stride=WIN), :] * column
            imag = plain[block, pl.ds(STA * WIN + window, STA, stride=WIN), :] * column
            for place, (near, far) in enumerate([(real, real), (imag, imag), (real + imag, real - imag)]):
                own_spec[block, place * WIN + window] = near
                far_spec[block, place * WIN + window] = far

    lane_in = lax.broadcasted_iota(jnp.int32, (LANES, LANES), 0)
    lane_out = lax.broadcasted_iota(jnp.int32, (LANES, LANES), 1)
    turned = lane_out // tile_rows * tile_rows + lane_out % STA * STA + lane_out % tile_rows // STA
    swap = (lane_in == turned).astype(jnp.float32).astype(jnp.bfloat16)
    labels = [meta[pl.ds(chunk, blocks, stride=WIN), :] for chunk in range(STEPS // 2)]
    turned_labels = [
        jnp.dot(each.astype(jnp.bfloat16), swap, preferred_element_type=jnp.float32) for each in labels[1:]
    ]
    names[0], names[1] = labels[0], labels[1]
    names[2], names[3] = turned_labels[1], turned_labels[0]
    names[4], names[5] = pltpu.roll(labels[1], tile_rows, 1), pltpu.roll(turned_labels[1], tile_rows, 1)

    def name(kind, block):
        return names[kind, block % blocks : block % blocks + 1, :]

    source = lax.broadcasted_iota(jnp.int32, (sources, LANES), 0).astype(jnp.float32).astype(jnp.bfloat16)
    one, zero = jnp.ones((HALF_TILE, LANES), jnp.bfloat16), jnp.zeros((HALF_TILE, LANES), jnp.bfloat16)
    low = lax.broadcasted_iota(jnp.int32, (1, LANES), 1) < tile_rows
    half = blocks // 2
    pairs_of = [(name(0, block), jnp.where(low, -1.0, name(2, block - 2))) for block in range(blocks)]
    pairs_of += [(name(1, block), jnp.where(low, name(2, block - 3), name(3, block + half))) for block in range(half)]
    pairs_of += [
        (
            jnp.where(low, name(1, block), name(4, block + 1)),
            jnp.where(low, name(2, block - 3), name(5, block - 2)),
        )
        for block in range(half, blocks, 2)
    ]
    for chunk, both in enumerate(pairs_of):
        at = slice(chunk * LANES, (chunk + 1) * LANES)
        forth, back = [jnp.broadcast_to(each, (HALF_TILE, LANES)).astype(jnp.bfloat16) for each in both]
        for first in range(0, sources, HALF_TILE):
            here = source[first : first + HALF_TILE]
            own_rows, far_rows = jnp.where(here == forth, one, zero), jnp.where(here == back, one, zero)
            hot[first : first + HALF_TILE, at] = own_rows + far_rows
            hot[sources + first : sources + first + HALF_TILE, at] = own_rows - far_rows

    def row_of(block, step):
        if step < 2:
            return block * LANES + step * tile_rows
        if block < half:
            return (blocks + block) * LANES + (step - 2) * tile_rows
        return (blocks + half) * LANES + (block - half) * tile_rows

    for block in range(blocks):
        steps = STEPS // 2 + (block < blocks // 2)
        for near in range(0, STA, 2):
            own = [
                [
                    jnp.broadcast_to(own_spec[block, place, near + more : near + more + 1, :], (STA, LANES))
                    for place in range(3 * WIN)
                ]
                for more in range(2)
            ]
            for step in range(steps):
                far_block = (block - 1 - step) % blocks
                far = [far_spec[far_block, place] for place in range(3 * WIN)]
                rows = []
                for more in range(2):
                    sums = [
                        sum(own[more][place] * far[place] for place in range(kind * WIN, (kind + 1) * WIN))
                        for kind in range(3)
                    ]
                    real, imag = sums[0] + sums[1], sums[2] - sums[0] + sums[1]
                    factor = lax.rsqrt(jnp.maximum(real * real + imag * imag, 1.0))
                    rows.append((real * factor, imag * factor))
                real = jnp.concatenate([rows[0][0], rows[1][0]], axis=0).astype(jnp.bfloat16)
                imag = jnp.concatenate([rows[0][1], rows[1][1]], axis=0).astype(jnp.bfloat16)
                at = row_of(block, step) + near * STA
                phat[at : at + 2 * STA, :LANES] = real
                phat[at : at + 2 * STA, LANES:] = imag
    total[...] = jnp.dot(hot[...], phat[...], preferred_element_type=jnp.float32)
    lead_move.wait()
    order = peer_order(blocks, groups)
    for block in range(blocks):
        at = slice(block * VS_DEV, (block + 1) * VS_DEV)
        real, imag = total[at, :LANES], total[sources + block * VS_DEV : sources + (block + 1) * VS_DEV, LANES:]
        for group in range(groups):
            cosine, sine = lead_ref[group : group + 1, :], lead_ref[groups + group : groups + group + 1, :]
            out_ref[order.index(block * groups + group)] = jnp.concatenate(
                [real * cosine - imag * sine, real * sine + imag * cosine], axis=1
            ).astype(jnp.bfloat16)


def pairs(got, lead):
    blocks, groups = got.shape[0], lead.shape[1] // 2
    sources, rows = blocks * VS_DEV, blocks * STEPS * STA * STA * 7 // 12
    return pl.pallas_call(
        pair_kernel,
        out_shape=pltpu.VMEM((blocks * groups, VS_DEV, 2 * LANES), jnp.bfloat16),
        in_specs=[VMEM, pl.BlockSpec(memory_space=pltpu.HBM)],
        out_specs=VMEM,
        compiler_params=pltpu.CompilerParams(vmem_limit_bytes=KERNEL_VMEM),
        scratch_shapes=[
            pltpu.VMEM(lead.shape[1:], lead.dtype),
            pltpu.VMEM((blocks, SPEC_TILES * WIN + STA, LANES), jnp.float32),
            pltpu.VMEM((blocks * WIN + STA, LANES), jnp.float32),
            pltpu.VMEM((blocks, 3 * WIN, STA, LANES), jnp.float32),
            pltpu.VMEM((blocks, 3 * WIN, STA, LANES), jnp.float32),
            pltpu.VMEM((STEPS, blocks, LANES), jnp.float32),
            pltpu.VMEM((rows, 2 * LANES), jnp.bfloat16),
            pltpu.VMEM((2 * sources, rows), jnp.bfloat16),
            pltpu.VMEM((2 * sources, 2 * LANES), jnp.float32),
            pltpu.SemaphoreType.DMA,
        ],
    )(got, pltpu.with_memory_space_constraint(lead, pltpu.HBM))


def lag_kernel(bins_ref, wave_ref, turn_ref, out_ref):
    chunks = bins_ref.shape[0]
    rows = bins_ref[...].reshape(chunks * VS_DEV, 2 * LANES)
    twice = [jnp.concatenate([rows[:, part * LANES : (part + 1) * LANES]] * 2, axis=1) for part in range(2)]
    tiles = wave_ref.shape[0]
    mirror = LANES - 1 - lax.broadcasted_iota(jnp.int32, (VS_DEV, LANES), 1)
    for tile in range(tiles):
        real, imag = [jnp.dot(each, wave_ref[tile], preferred_element_type=jnp.float32) for each in twice]
        even, odd = jnp.zeros((VS_DEV, LANES), jnp.float32), jnp.zeros((VS_DEV, LANES), jnp.float32)
        for chunk in range(chunks):
            at = slice(chunk * VS_DEV, (chunk + 1) * VS_DEV)
            cosine, sine = turn_ref[0, chunk : chunk + 1, :], turn_ref[1, chunk : chunk + 1, :]
            even += real[at, :LANES] * cosine - real[at, LANES:] * sine
            odd += imag[at, :LANES] * sine + imag[at, LANES:] * cosine
        after, before = tiles + tile, tiles - 1 - tile
        out_ref[:, after * LANES : (after + 1) * LANES] = even - odd
        out_ref[:, before * LANES : (before + 1) * LANES] = jnp.take_along_axis(even + odd, mirror, axis=1)


def lags_of(bins, wave, turn):
    return pl.pallas_call(
        lag_kernel,
        out_shape=jax.ShapeDtypeStruct((VS_DEV, 2 * wave.shape[0] * LANES), jnp.float32),
        in_specs=[VMEM] * 3,
        out_specs=VMEM,
        compiler_params=pltpu.CompilerParams(vmem_limit_bytes=KERNEL_VMEM),
    )(bins, wave, turn)


def turns(phase):
    angle = np.mod(phase, 2 * BINS) * (math.pi / BINS)
    return np.cos(angle), np.sin(angle)


def lag_tables(blocks, groups):
    lag_dev = LAGS // groups
    chunks = blocks * groups
    middle = np.arange(groups) * lag_dev - LAGS // 2 + (lag_dev - 1) / 2
    bins = np.arange(LANES)
    whole = LANES * np.arange(chunks)[:, None, None] + bins
    lead = np.concatenate(turns(whole * middle[:, None]), axis=1).astype(np.float32)
    tiles = []
    for first in range(0, lag_dev // 2, LANES):
        tiles.append(np.concatenate(turns(bins[:, None] * (first + bins + 0.5)), axis=1))
    wave = np.stack(tiles) / math.sqrt(BINS)
    high = wave.astype(jnp.bfloat16)
    low = (wave - high.astype(np.float64)).astype(jnp.bfloat16)
    place = np.array(peer_order(blocks, groups))
    chunk = place % groups * blocks + place // groups
    turn = np.stack(turns(LANES * chunk[:, None] * (bins + 0.5))).astype(np.float32)
    return jnp.asarray(lead), jnp.asarray(np.concatenate([high, low], axis=1)), jnp.asarray(turn)


def peer_order(blocks, groups):
    first = [0, groups]
    return first + [device for device in range(blocks * groups) if device not in first]


def by_bins(spectra, quality, pair_mask, owners, local_rows):
    blocks, groups = lax.axis_size("blk"), lax.axis_size("grp")
    lead, wave, turn = lag_tables(blocks, groups)
    sent = pack(spectra, quality, pair_mask, owners, local_rows, blocks)
    got = lax.all_to_all(sent, "blk", split_axis=0, concat_axis=0, tiled=True)
    summed = pairs(got, lead)
    order = [peer_order(blocks, groups)]
    bins = lax.all_to_all(
        summed, ("blk", "grp"), split_axis=0, concat_axis=0, tiled=True, axis_index_groups=order
    )
    return lags_of(bins, wave, turn)


def from_behind(array, axis, by):
    size = lax.axis_size(axis)
    return lax.ppermute(array, axis, [(i, (i + by) % size) for i in range(size)])


def lag_table(bins_index, total_bins, lags):
    shifts = jnp.arange(lags, dtype=jnp.int32) - lags // 2
    phase = jnp.mod(bins_index[:, None] * shifts[None, :], 2 * total_bins)
    angle = phase.astype(jnp.float32) * (math.pi / total_bins)
    factor = 1.0 / math.sqrt(total_bins)
    return jnp.concatenate([jnp.cos(angle) * factor, -jnp.sin(angle) * factor], axis=0).astype(
        jnp.bfloat16
    )


def phase_rows(own_spec, own_weight, far_spec, far_weight, sub_mask):
    near_weight = own_weight.astype(jnp.float32)[:, :, None]
    away_weight = far_weight.astype(jnp.float32)[:, :, None]
    a_real = own_spec[0].astype(jnp.float32) * near_weight
    a_imag = own_spec[1].astype(jnp.float32) * near_weight
    b_real = far_spec[0].astype(jnp.float32) * away_weight
    b_imag = far_spec[1].astype(jnp.float32) * away_weight
    cross_real = jnp.sum(a_real[:, None] * b_real[None] + a_imag[:, None] * b_imag[None], axis=2)
    cross_imag = jnp.sum(a_imag[:, None] * b_real[None] - a_real[:, None] * b_imag[None], axis=2)
    station_mask = jnp.repeat(jnp.repeat(sub_mask, SUB, axis=0), SUB, axis=1).astype(jnp.float32)
    factor = station_mask[:, :, None] * lax.rsqrt(
        jnp.maximum(cross_real * cross_real + cross_imag * cross_imag, 1.0)
    )
    joined = jnp.concatenate([cross_real * factor, cross_imag * factor], axis=2).astype(
        jnp.bfloat16
    )
    return joined.reshape(STA * STA, joined.shape[2])


def by_halo(spectra, quality, pair_mask, owners, local_rows):
    bins_dev = spectra.shape[3]
    blocks = lax.axis_size("blk")
    rows_dev = owners.shape[0]
    capacity = max(2, 2 * rows_dev // blocks)
    masks = pair_mask[0]
    pieces = [None] * STEPS
    visiting = (spectra, quality)
    for offset in range(STEPS):
        visiting = from_behind((visiting[0], visiting[1]), "blk", 1)
        pieces[offset] = phase_rows(spectra, quality, visiting[0], visiting[1], masks[offset])
    rows_all = jnp.concatenate(pieces, axis=0)
    owner_flat = owners[:, 0]
    row_index = jnp.arange(rows_dev, dtype=jnp.int32)
    earlier = (owner_flat[:, None] == owner_flat[None, :]) & (
        row_index[None, :] < row_index[:, None]
    )
    position = jnp.sum(earlier.astype(jnp.int32), axis=1)
    slot_index = owner_flat * capacity + position
    sources = jnp.arange(VS_DEV, dtype=jnp.int32)
    bins_index = lax.axis_index("grp") * bins_dev + jnp.arange(bins_dev, dtype=jnp.int32)
    table = lag_table(bins_index, BINS, LAGS)
    lag_dev = LAGS // lax.axis_size("grp")
    lag_terms = lax.psum_scatter(
        lax.dot_general(
            table, rows_all, (((0,), (1,)), ((), ())), preferred_element_type=jnp.float32
        ),
        "grp",
        scatter_dimension=0,
        tiled=True,
    )
    outgoing = jnp.zeros((lag_dev, blocks * capacity), jnp.float32).at[:, slot_index].set(lag_terms)
    labels = jnp.full((1, blocks * capacity), -1, jnp.int32).at[0, slot_index].set(local_rows)
    received, got_labels = (
        lax.all_to_all(outgoing, "blk", split_axis=1, concat_axis=1, tiled=True),
        lax.all_to_all(labels, "blk", split_axis=1, concat_axis=1, tiled=True),
    )
    selector = (got_labels == sources[:, None]).astype(jnp.float32)
    stack = lax.dot_general(
        selector,
        received,
        (((1,), (1,)), ((), ())),
        precision=lax.Precision.HIGHEST,
        preferred_element_type=jnp.float32,
    )
    return stack


def on_device(spectra, quality, pair_mask, owners, local_rows):
    blocks, groups = lax.axis_size("blk"), lax.axis_size("grp")
    whole_tiles = spectra.shape[3] == blocks * LANES and LAGS // groups % (2 * LANES) == 0
    if whole_tiles and blocks == STEPS + 2:
        return by_bins(spectra, quality, pair_mask, owners, local_rows)
    return by_halo(spectra, quality, pair_mask, owners, local_rows)


def solution(mesh):
    in_specs = (
        P(None, "blk", None, "grp"),
        P("blk", None),
        P("blk", None, None, None),
        P("blk", None),
        P("blk"),
    )
    out_specs = P("blk", "grp")
    return jax.shard_map(
        on_device, mesh=mesh, in_specs=in_specs, out_specs=out_specs, check_vma=False
    )
```

```python
import math

import jax
import jax.numpy as jnp
import numpy as np
from jax import lax
from jax.experimental import pallas as pl
from jax.experimental.pallas import tpu as pltpu
from jax.sharding import PartitionSpec as P

STA = 8
WIN = 4
BINS = 4096
LAGS = 2048
STEPS = 6
SUB = 4
VS_DEV = 16
LANES = 128
SPEC_TILES = 2 * STA
HALF_TILE = 16
KERNEL_VMEM = 12 * 1024 * 1024

VMEM = pl.BlockSpec(memory_space=pltpu.VMEM)


def pack_kernel(spec_hbm, weight_hbm, mask_hbm, owner_hbm, local_hbm, out_ref, weight_ref, mask_ref, owner_ref, local_ref, sliced, arrived):
    dests = out_ref.shape[0]
    slices = [
        pltpu.make_async_copy(
            spec_hbm.at[:, :, pl.ds(dest * LANES, LANES)],
            out_ref.at[dest, pl.ds(0, SPEC_TILES)],
            sliced.at[dest],
        )
        for dest in range(dests)
    ]
    small = [(weight_hbm, weight_ref), (mask_hbm, mask_ref), (owner_hbm, owner_ref), (local_hbm, local_ref)]
    moves = [
        pltpu.make_async_copy(source, target, arrived.at[place])
        for place, (source, target) in enumerate(small)
    ]
    for move in moves + slices:
        move.start()
    lane = lax.broadcasted_iota(jnp.int32, (1, LANES), 1)
    for move in moves:
        move.wait()
    rows = []
    for chunk in range(STEPS // 2):
        part = slice(chunk * LANES, (chunk + 1) * LANES)
        mask = jnp.zeros((1, LANES), jnp.int32)
        for odd in range(2):
            for near in range(2):
                for far in range(2):
                    here = (lane // 64 == odd) & (lane % 64 // 32 == near) & (lane % 8 // 4 == far)
                    step = chunk * 2 + odd
                    mask = jnp.where(here, mask_ref[near, far : far + 1, step : step + 1], mask)
        source = owner_ref[:, part] * VS_DEV + local_ref[part].reshape(1, LANES)
        rows.append(jnp.where(mask != 0, source, -1).astype(jnp.float32))
    weights = [weight_ref[window : window + 1, :].astype(jnp.float32) for window in range(WIN)]
    rows.append(jnp.concatenate(weights + [jnp.zeros((1, LANES - WIN * STA), jnp.float32)], axis=1))
    meta = jnp.concatenate(rows, axis=0).astype(jnp.bfloat16)
    for dest in range(dests):
        out_ref[dest, SPEC_TILES] = meta
    for move in slices:
        move.wait()


def pack(spectra, quality, pair_mask, owners, local_rows, blocks):
    rows = owners.shape[0]
    operands = (
        spectra.reshape(SPEC_TILES, WIN, spectra.shape[3]),
        quality.T,
        pair_mask[0].transpose(1, 2, 0),
        owners.reshape(1, rows),
        local_rows,
    )
    return pl.pallas_call(
        pack_kernel,
        out_shape=pltpu.VMEM((blocks, SPEC_TILES + 1, WIN, LANES), jnp.bfloat16),
        in_specs=[pl.BlockSpec(memory_space=pltpu.HBM)] * len(operands),
        out_specs=VMEM,
        compiler_params=pltpu.CompilerParams(vmem_limit_bytes=KERNEL_VMEM),
        scratch_shapes=[pltpu.VMEM(each.shape, each.dtype) for each in operands[1:]]
        + [pltpu.SemaphoreType.DMA((blocks,)), pltpu.SemaphoreType.DMA((len(operands) - 1,))],
    )(*[pltpu.with_memory_space_constraint(each, pltpu.HBM) for each in operands])


def pair_kernel(got_ref, lead_hbm, out_ref, lead_ref, plain, meta, own_spec, far_spec, names, phat, hot, total, arrived):
    blocks = got_ref.shape[0]
    groups = out_ref.shape[0] // blocks
    sources = blocks * VS_DEV
    tile_rows = STA * STA
    chunk_here = lax.axis_index("grp") * blocks + lax.axis_index("blk")
    lead_move = pltpu.make_async_copy(lead_hbm.at[chunk_here], lead_ref, arrived)
    lead_move.start()

    for block in range(blocks):
        for tile in range(SPEC_TILES):
            plain[block, tile * WIN : (tile + 1) * WIN, :] = got_ref[block, tile].astype(jnp.float32)
        meta[block * WIN : (block + 1) * WIN, :] = got_ref[block, SPEC_TILES].astype(jnp.float32)
    weights = meta[pl.ds(WIN - 1, blocks, stride=WIN), :]
    station_of = lax.broadcasted_iota(jnp.int32, (STA, LANES), 0)
    on_lane = lax.broadcasted_iota(jnp.int32, (STA, LANES), 1)
    for block in range(blocks):
        for window in range(WIN):
            mine = jnp.where(on_lane == window * STA + station_of, weights[block : block + 1, :], 0.0)
            column = jnp.sum(mine, axis=1, keepdims=True)
            real = plain[block, pl.ds(window, STA, stride=WIN), :] * column
            imag = plain[block, pl.ds(STA * WIN + window, STA, stride=WIN), :] * column
            for place, (near, far) in enumerate([(real + imag, real), (real, real + imag), (imag, real - imag)]):
                own_spec[block, place * WIN + window] = near
                far_spec[block, place * WIN + window] = far

    lane_in = lax.broadcasted_iota(jnp.int32, (LANES, LANES), 0)
    lane_out = lax.broadcasted_iota(jnp.int32, (LANES, LANES), 1)
    turned = lane_out // tile_rows * tile_rows + lane_out % STA * STA + lane_out % tile_rows // STA
    swap = (lane_in == turned).astype(jnp.float32).astype(jnp.bfloat16)
    labels = [meta[pl.ds(chunk, blocks, stride=WIN), :] for chunk in range(STEPS // 2)]
    turned_labels = [
        jnp.dot(each.astype(jnp.bfloat16), swap, preferred_element_type=jnp.float32) for each in labels[1:]
    ]
    names[0], names[1] = labels[0], labels[1]
    names[2], names[3] = turned_labels[1], turned_labels[0]
    names[4], names[5] = pltpu.roll(labels[1], tile_rows, 1), pltpu.roll(turned_labels[1], tile_rows, 1)

    def name(kind, block):
        return names[kind, block % blocks : block % blocks + 1, :]

    source = lax.broadcasted_iota(jnp.int32, (sources, LANES), 0).astype(jnp.float32).astype(jnp.bfloat16)
    one, zero = jnp.ones((HALF_TILE, LANES), jnp.bfloat16), jnp.zeros((HALF_TILE, LANES), jnp.bfloat16)
    low = lax.broadcasted_iota(jnp.int32, (1, LANES), 1) < tile_rows
    half = blocks // 2
    pairs_of = [(name(0, block), jnp.where(low, -1.0, name(2, block - 2))) for block in range(blocks)]
    pairs_of += [(name(1, block), jnp.where(low, name(2, block - 3), name(3, block + half))) for block in range(half)]
    pairs_of += [
        (
            jnp.where(low, name(1, block), name(4, block + 1)),
            jnp.where(low, name(2, block - 3), name(5, block - 2)),
        )
        for block in range(half, blocks, 2)
    ]
    for chunk, both in enumerate(pairs_of):
        at = slice(chunk * LANES, (chunk + 1) * LANES)
        forth, back = [jnp.broadcast_to(each, (HALF_TILE, LANES)).astype(jnp.bfloat16) for each in both]
        for first in range(0, sources, HALF_TILE):
            here = source[first : first + HALF_TILE]
            own_rows, far_rows = jnp.where(here == forth, one, zero), jnp.where(here == back, one, zero)
            hot[first : first + HALF_TILE, at] = own_rows + far_rows
            hot[sources + first : sources + first + HALF_TILE, at] = own_rows - far_rows

    def row_of(block, step):
        if step < 2:
            return block * LANES + step * tile_rows
        if block < half:
            return (blocks + block) * LANES + (step - 2) * tile_rows
        return (blocks + half) * LANES + (block - half) * tile_rows

    for block in range(blocks):
        steps = STEPS // 2 + (block < blocks // 2)
        for near in range(0, STA, 2):
            own = [
                [
                    jnp.broadcast_to(own_spec[block, place, near + more : near + more + 1, :], (STA, LANES))
                    for place in range(3 * WIN)
                ]
                for more in range(2)
            ]
            for step in range(steps):
                far_block = (block - 1 - step) % blocks
                far = [far_spec[far_block, place] for place in range(3 * WIN)]
                rows = []
                for more in range(2):
                    sums = [
                        sum(own[more][place] * far[place] for place in range(kind * WIN, (kind + 1) * WIN))
                        for kind in range(3)
                    ]
                    real, imag = sums[0] - sums[2], sums[0] - sums[1]
                    factor = lax.rsqrt(jnp.maximum(real * real + imag * imag, 1.0))
                    rows.append((real * factor, imag * factor))
                real = jnp.concatenate([rows[0][0], rows[1][0]], axis=0).astype(jnp.bfloat16)
                imag = jnp.concatenate([rows[0][1], rows[1][1]], axis=0).astype(jnp.bfloat16)
                at = row_of(block, step) + near * STA
                phat[at : at + 2 * STA, :LANES] = real
                phat[at : at + 2 * STA, LANES:] = imag
    total[...] = jnp.dot(hot[...], phat[...], preferred_element_type=jnp.float32)
    lead_move.wait()
    for block in range(blocks):
        at = slice(block * VS_DEV, (block + 1) * VS_DEV)
        real, imag = total[at, :LANES], total[sources + block * VS_DEV : sources + (block + 1) * VS_DEV, LANES:]
        for group in range(groups):
            cosine, sine = lead_ref[group : group + 1, :], lead_ref[groups + group : groups + group + 1, :]
            out_ref[block * groups + group] = jnp.concatenate(
                [real * cosine - imag * sine, real * sine + imag * cosine], axis=1
            ).astype(jnp.bfloat16)


def pairs(got, lead):
    blocks, groups = got.shape[0], lead.shape[1] // 2
    sources, rows = blocks * VS_DEV, blocks * STEPS * STA * STA * 7 // 12
    return pl.pallas_call(
        pair_kernel,
        out_shape=pltpu.VMEM((blocks * groups, VS_DEV, 2 * LANES), jnp.bfloat16),
        in_specs=[VMEM, pl.BlockSpec(memory_space=pltpu.HBM)],
        out_specs=VMEM,
        compiler_params=pltpu.CompilerParams(vmem_limit_bytes=KERNEL_VMEM),
        scratch_shapes=[
            pltpu.VMEM(lead.shape[1:], lead.dtype),
            pltpu.VMEM((blocks, SPEC_TILES * WIN + STA, LANES), jnp.float32),
            pltpu.VMEM((blocks * WIN + STA, LANES), jnp.float32),
            pltpu.VMEM((blocks, 3 * WIN, STA, LANES), jnp.float32),
            pltpu.VMEM((blocks, 3 * WIN, STA, LANES), jnp.float32),
            pltpu.VMEM((STEPS, blocks, LANES), jnp.float32),
            pltpu.VMEM((rows, 2 * LANES), jnp.bfloat16),
            pltpu.VMEM((2 * sources, rows), jnp.bfloat16),
            pltpu.VMEM((2 * sources, 2 * LANES), jnp.float32),
            pltpu.SemaphoreType.DMA,
        ],
    )(got, pltpu.with_memory_space_constraint(lead, pltpu.HBM))


def lag_kernel(bins_ref, wave_ref, turn_ref, out_ref):
    chunks = bins_ref.shape[0]
    rows = bins_ref[...].reshape(chunks * VS_DEV, 2 * LANES)
    twice = [jnp.concatenate([rows[:, part * LANES : (part + 1) * LANES]] * 2, axis=1) for part in range(2)]
    tiles = wave_ref.shape[0]
    mirror = LANES - 1 - lax.broadcasted_iota(jnp.int32, (VS_DEV, LANES), 1)
    for tile in range(tiles):
        real, imag = [jnp.dot(each, wave_ref[tile], preferred_element_type=jnp.float32) for each in twice]
        even, odd = jnp.zeros((VS_DEV, LANES), jnp.float32), jnp.zeros((VS_DEV, LANES), jnp.float32)
        for chunk in range(chunks):
            at = slice(chunk * VS_DEV, (chunk + 1) * VS_DEV)
            cosine, sine = turn_ref[0, chunk : chunk + 1, :], turn_ref[1, chunk : chunk + 1, :]
            even += real[at, :LANES] * cosine - real[at, LANES:] * sine
            odd += imag[at, :LANES] * sine + imag[at, LANES:] * cosine
        after, before = tiles + tile, tiles - 1 - tile
        out_ref[:, after * LANES : (after + 1) * LANES] = even - odd
        out_ref[:, before * LANES : (before + 1) * LANES] = jnp.take_along_axis(even + odd, mirror, axis=1)


def lags_of(bins, wave, turn):
    return pl.pallas_call(
        lag_kernel,
        out_shape=jax.ShapeDtypeStruct((VS_DEV, 2 * wave.shape[0] * LANES), jnp.float32),
        in_specs=[VMEM] * 3,
        out_specs=VMEM,
        compiler_params=pltpu.CompilerParams(vmem_limit_bytes=KERNEL_VMEM),
    )(bins, wave, turn)


def turns(phase):
    angle = np.mod(phase, 2 * BINS) * (math.pi / BINS)
    return np.cos(angle), np.sin(angle)


def lag_tables(blocks, groups):
    lag_dev = LAGS // groups
    chunks = blocks * groups
    middle = np.arange(groups) * lag_dev - LAGS // 2 + (lag_dev - 1) / 2
    bins = np.arange(LANES)
    whole = LANES * np.arange(chunks)[:, None, None] + bins
    lead = np.concatenate(turns(whole * middle[:, None]), axis=1).astype(np.float32)
    tiles = []
    for first in range(0, lag_dev // 2, LANES):
        tiles.append(np.concatenate(turns(bins[:, None] * (first + bins + 0.5)), axis=1))
    wave = np.stack(tiles) / math.sqrt(BINS)
    high = wave.astype(jnp.bfloat16)
    low = (wave - high.astype(np.float64)).astype(jnp.bfloat16)
    place = np.arange(chunks)
    chunk = place % groups * blocks + place // groups
    turn = np.stack(turns(LANES * chunk[:, None] * (bins + 0.5))).astype(np.float32)
    return jnp.asarray(lead), jnp.asarray(np.concatenate([high, low], axis=1)), jnp.asarray(turn)


def by_bins(spectra, quality, pair_mask, owners, local_rows):
    blocks, groups = lax.axis_size("blk"), lax.axis_size("grp")
    lead, wave, turn = lag_tables(blocks, groups)
    sent = pack(spectra, quality, pair_mask, owners, local_rows, blocks)
    got = lax.all_to_all(sent, "blk", split_axis=0, concat_axis=0, tiled=True)
    summed = pairs(got, lead)
    bins = lax.all_to_all(summed, ("blk", "grp"), split_axis=0, concat_axis=0, tiled=True)
    return lags_of(bins, wave, turn)


def from_behind(array, axis, by):
    size = lax.axis_size(axis)
    return lax.ppermute(array, axis, [(i, (i + by) % size) for i in range(size)])


def lag_table(bins_index, total_bins, lags):
    shifts = jnp.arange(lags, dtype=jnp.int32) - lags // 2
    phase = jnp.mod(bins_index[:, None] * shifts[None, :], 2 * total_bins)
    angle = phase.astype(jnp.float32) * (math.pi / total_bins)
    factor = 1.0 / math.sqrt(total_bins)
    return jnp.concatenate([jnp.cos(angle) * factor, -jnp.sin(angle) * factor], axis=0).astype(
        jnp.bfloat16
    )


def phase_rows(own_spec, own_weight, far_spec, far_weight, sub_mask):
    near_weight = own_weight.astype(jnp.float32)[:, :, None]
    away_weight = far_weight.astype(jnp.float32)[:, :, None]
    a_real = own_spec[0].astype(jnp.float32) * near_weight
    a_imag = own_spec[1].astype(jnp.float32) * near_weight
    b_real = far_spec[0].astype(jnp.float32) * away_weight
    b_imag = far_spec[1].astype(jnp.float32) * away_weight
    cross_real = jnp.sum(a_real[:, None] * b_real[None] + a_imag[:, None] * b_imag[None], axis=2)
    cross_imag = jnp.sum(a_imag[:, None] * b_real[None] - a_real[:, None] * b_imag[None], axis=2)
    station_mask = jnp.repeat(jnp.repeat(sub_mask, SUB, axis=0), SUB, axis=1).astype(jnp.float32)
    factor = station_mask[:, :, None] * lax.rsqrt(
        jnp.maximum(cross_real * cross_real + cross_imag * cross_imag, 1.0)
    )
    joined = jnp.concatenate([cross_real * factor, cross_imag * factor], axis=2).astype(
        jnp.bfloat16
    )
    return joined.reshape(STA * STA, joined.shape[2])


def by_halo(spectra, quality, pair_mask, owners, local_rows):
    bins_dev = spectra.shape[3]
    blocks = lax.axis_size("blk")
    rows_dev = owners.shape[0]
    capacity = max(2, 2 * rows_dev // blocks)
    masks = pair_mask[0]
    pieces = [None] * STEPS
    visiting = (spectra, quality)
    for offset in range(STEPS):
        visiting = from_behind((visiting[0], visiting[1]), "blk", 1)
        pieces[offset] = phase_rows(spectra, quality, visiting[0], visiting[1], masks[offset])
    rows_all = jnp.concatenate(pieces, axis=0)
    owner_flat = owners[:, 0]
    row_index = jnp.arange(rows_dev, dtype=jnp.int32)
    earlier = (owner_flat[:, None] == owner_flat[None, :]) & (
        row_index[None, :] < row_index[:, None]
    )
    position = jnp.sum(earlier.astype(jnp.int32), axis=1)
    slot_index = owner_flat * capacity + position
    sources = jnp.arange(VS_DEV, dtype=jnp.int32)
    bins_index = lax.axis_index("grp") * bins_dev + jnp.arange(bins_dev, dtype=jnp.int32)
    table = lag_table(bins_index, BINS, LAGS)
    lag_dev = LAGS // lax.axis_size("grp")
    lag_terms = lax.psum_scatter(
        lax.dot_general(
            table, rows_all, (((0,), (1,)), ((), ())), preferred_element_type=jnp.float32
        ),
        "grp",
        scatter_dimension=0,
        tiled=True,
    )
    outgoing = jnp.zeros((lag_dev, blocks * capacity), jnp.float32).at[:, slot_index].set(lag_terms)
    labels = jnp.full((1, blocks * capacity), -1, jnp.int32).at[0, slot_index].set(local_rows)
    received, got_labels = (
        lax.all_to_all(outgoing, "blk", split_axis=1, concat_axis=1, tiled=True),
        lax.all_to_all(labels, "blk", split_axis=1, concat_axis=1, tiled=True),
    )
    selector = (got_labels == sources[:, None]).astype(jnp.float32)
    stack = lax.dot_general(
        selector,
        received,
        (((1,), (1,)), ((), ())),
        precision=lax.Precision.HIGHEST,
        preferred_element_type=jnp.float32,
    )
    return stack


def on_device(spectra, quality, pair_mask, owners, local_rows):
    blocks, groups = lax.axis_size("blk"), lax.axis_size("grp")
    whole_tiles = spectra.shape[3] == blocks * LANES and LAGS // groups % (2 * LANES) == 0
    if whole_tiles and blocks == STEPS + 2:
        return by_bins(spectra, quality, pair_mask, owners, local_rows)
    return by_halo(spectra, quality, pair_mask, owners, local_rows)


def solution(mesh):
    in_specs = (
        P(None, "blk", None, "grp"),
        P("blk", None),
        P("blk", None, None, None),
        P("blk", None),
        P("blk"),
    )
    out_specs = P("blk", "grp")
    return jax.shard_map(
        on_device, mesh=mesh, in_specs=in_specs, out_specs=out_specs, check_vma=False
    )
```

```python
import math

import jax
import jax.numpy as jnp
import numpy as np
from jax import lax
from jax.experimental import pallas as pl
from jax.experimental.pallas import tpu as pltpu
from jax.sharding import PartitionSpec as P

STA = 8
WIN = 4
BINS = 4096
LAGS = 2048
STEPS = 6
SUB = 4
VS_DEV = 16
LANES = 128
SPEC_TILES = 2 * STA
HALF_TILE = 16
KERNEL_VMEM = 12 * 1024 * 1024

VMEM = pl.BlockSpec(memory_space=pltpu.VMEM)


def pack_kernel(spec_hbm, weight_hbm, mask_hbm, owner_hbm, local_hbm, out_ref, weight_ref, mask_ref, owner_ref, local_ref, sliced, arrived):
    dests = out_ref.shape[0]
    slices = [
        pltpu.make_async_copy(
            spec_hbm.at[:, :, pl.ds(dest * LANES, LANES)],
            out_ref.at[dest, pl.ds(0, SPEC_TILES)],
            sliced.at[dest],
        )
        for dest in range(dests)
    ]
    small = [(weight_hbm, weight_ref), (mask_hbm, mask_ref), (owner_hbm, owner_ref), (local_hbm, local_ref)]
    moves = [
        pltpu.make_async_copy(source, target, arrived.at[place])
        for place, (source, target) in enumerate(small)
    ]
    for move in moves + slices:
        move.start()
    lane = lax.broadcasted_iota(jnp.int32, (1, LANES), 1)
    for move in moves:
        move.wait()
    rows = []
    for chunk in range(STEPS // 2):
        part = slice(chunk * LANES, (chunk + 1) * LANES)
        mask = jnp.zeros((1, LANES), jnp.int32)
        for odd in range(2):
            for near in range(2):
                for far in range(2):
                    here = (lane // 64 == odd) & (lane % 64 // 32 == near) & (lane % 8 // 4 == far)
                    step = chunk * 2 + odd
                    mask = jnp.where(here, mask_ref[near, far : far + 1, step : step + 1], mask)
        source = owner_ref[:, part] * VS_DEV + local_ref[part].reshape(1, LANES)
        rows.append(jnp.where(mask != 0, source, -1).astype(jnp.float32))
    weights = [weight_ref[window : window + 1, :].astype(jnp.float32) for window in range(WIN)]
    rows.append(jnp.concatenate(weights + [jnp.zeros((1, LANES - WIN * STA), jnp.float32)], axis=1))
    meta = jnp.concatenate(rows, axis=0).astype(jnp.bfloat16)
    for dest in range(dests):
        out_ref[dest, SPEC_TILES] = meta
    for move in slices:
        move.wait()


def pack(spectra, quality, pair_mask, owners, local_rows, blocks):
    rows = owners.shape[0]
    operands = (
        spectra.reshape(SPEC_TILES, WIN, spectra.shape[3]),
        quality.T,
        pair_mask[0].transpose(1, 2, 0),
        owners.reshape(1, rows),
        local_rows,
    )
    return pl.pallas_call(
        pack_kernel,
        out_shape=pltpu.VMEM((blocks, SPEC_TILES + 1, WIN, LANES), jnp.bfloat16),
        in_specs=[pl.BlockSpec(memory_space=pltpu.HBM)] * len(operands),
        out_specs=VMEM,
        compiler_params=pltpu.CompilerParams(vmem_limit_bytes=KERNEL_VMEM),
        scratch_shapes=[pltpu.VMEM(each.shape, each.dtype) for each in operands[1:]]
        + [pltpu.SemaphoreType.DMA((blocks,)), pltpu.SemaphoreType.DMA((len(operands) - 1,))],
    )(*[pltpu.with_memory_space_constraint(each, pltpu.HBM) for each in operands])


def pair_kernel(got_ref, lead_hbm, out_ref, lead_ref, plain, meta, own_spec, far_spec, names, phat, hot, total, arrived):
    blocks = got_ref.shape[0]
    groups = out_ref.shape[0] // blocks
    sources = blocks * VS_DEV
    tile_rows = STA * STA
    chunk_here = lax.axis_index("grp") * blocks + lax.axis_index("blk")
    lead_move = pltpu.make_async_copy(lead_hbm.at[chunk_here], lead_ref, arrived)
    lead_move.start()

    for block in range(blocks):
        for tile in range(SPEC_TILES):
            plain[block, tile * WIN : (tile + 1) * WIN, :] = got_ref[block, tile].astype(jnp.float32)
        meta[block * WIN : (block + 1) * WIN, :] = got_ref[block, SPEC_TILES].astype(jnp.float32)
    weights = meta[pl.ds(WIN - 1, blocks, stride=WIN), :]
    station_of = lax.broadcasted_iota(jnp.int32, (STA, LANES), 0)
    on_lane = lax.broadcasted_iota(jnp.int32, (STA, LANES), 1)
    for block in range(blocks):
        for window in range(WIN):
            mine = jnp.where(on_lane == window * STA + station_of, weights[block : block + 1, :], 0.0)
            column = jnp.sum(mine, axis=1, keepdims=True)
            real = plain[block, pl.ds(window, STA, stride=WIN), :] * column
            imag = plain[block, pl.ds(STA * WIN + window, STA, stride=WIN), :] * column
            for place, (near, far) in enumerate([(real, real), (imag, imag), (real + imag, real - imag)]):
                own_spec[block, place * WIN + window] = near
                far_spec[block, place * WIN + window] = far

    lane_in = lax.broadcasted_iota(jnp.int32, (LANES, LANES), 0)
    lane_out = lax.broadcasted_iota(jnp.int32, (LANES, LANES), 1)
    turned = lane_out // tile_rows * tile_rows + lane_out % STA * STA + lane_out % tile_rows // STA
    swap = (lane_in == turned).astype(jnp.float32).astype(jnp.bfloat16)
    labels = [meta[pl.ds(chunk, blocks, stride=WIN), :] for chunk in range(STEPS // 2)]
    turned_labels = [
        jnp.dot(each.astype(jnp.bfloat16), swap, preferred_element_type=jnp.float32) for each in labels[1:]
    ]
    names[0], names[1] = labels[0], labels[1]
    names[2], names[3] = turned_labels[1], turned_labels[0]
    names[4], names[5] = pltpu.roll(labels[1], tile_rows, 1), pltpu.roll(turned_labels[1], tile_rows, 1)

    def name(kind, block):
        return names[kind, block % blocks : block % blocks + 1, :]

    source = lax.broadcasted_iota(jnp.int32, (sources, LANES), 0).astype(jnp.float32).astype(jnp.bfloat16)
    one, zero = jnp.ones((HALF_TILE, LANES), jnp.bfloat16), jnp.zeros((HALF_TILE, LANES), jnp.bfloat16)
    low = lax.broadcasted_iota(jnp.int32, (1, LANES), 1) < tile_rows
    half = blocks // 2
    pairs_of = []
    for block in range(blocks):
        pairs_of.append((name(0, block), jnp.where(low, -1.0, name(2, block - 2))))
        if block < half:
            pairs_of.append((name(1, block), jnp.where(low, name(2, block - 3), name(3, block + half))))
    pairs_of += [
        (
            jnp.where(low, name(1, block), name(4, block + 1)),
            jnp.where(low, name(2, block - 3), name(5, block - 2)),
        )
        for block in range(half, blocks, 2)
    ]
    for chunk, both in enumerate(pairs_of):
        at = slice(chunk * LANES, (chunk + 1) * LANES)
        forth, back = [jnp.broadcast_to(each, (HALF_TILE, LANES)).astype(jnp.bfloat16) for each in both]
        for first in range(0, sources, HALF_TILE):
            here = source[first : first + HALF_TILE]
            own_rows, far_rows = jnp.where(here == forth, one, zero), jnp.where(here == back, one, zero)
            hot[first : first + HALF_TILE, at] = own_rows + far_rows
            hot[sources + first : sources + first + HALF_TILE, at] = own_rows - far_rows

    def row_of(block, step):
        if block < half:
            return 2 * block * LANES + step * tile_rows
        if step < 2:
            return (block + half) * LANES + step * tile_rows
        return (blocks + half) * LANES + (block - half) * tile_rows

    for block in range(blocks):
        steps = STEPS // 2 + (block < blocks // 2)
        for near in range(0, STA, 2):
            own = [
                [
                    jnp.broadcast_to(own_spec[block, place, near + more : near + more + 1, :], (STA, LANES))
                    for place in range(3 * WIN)
                ]
                for more in range(2)
            ]
            for step in range(steps):
                far_block = (block - 1 - step) % blocks
                far = [far_spec[far_block, place] for place in range(3 * WIN)]
                rows = []
                for more in range(2):
                    sums = [
                        sum(own[more][place] * far[place] for place in range(kind * WIN, (kind + 1) * WIN))
                        for kind in range(3)
                    ]
                    real, imag = sums[0] + sums[1], sums[2] - sums[0] + sums[1]
                    factor = lax.rsqrt(jnp.maximum(real * real + imag * imag, 1.0))
                    rows.append((real * factor, imag * factor))
                real = jnp.concatenate([rows[0][0], rows[1][0]], axis=0).astype(jnp.bfloat16)
                imag = jnp.concatenate([rows[0][1], rows[1][1]], axis=0).astype(jnp.bfloat16)
                at = row_of(block, step) + near * STA
                phat[at : at + 2 * STA, :LANES] = real
                phat[at : at + 2 * STA, LANES:] = imag
        if block == half:
            both = jnp.dot(hot[:, :1024], phat[:1024, :], preferred_element_type=jnp.float32)
            total[0] = both[:sources, :LANES]
            total[1] = both[sources:, LANES:]
    both = jnp.dot(hot[:, 1024:], phat[1024:, :], preferred_element_type=jnp.float32)
    total[0] += both[:sources, :LANES]
    total[1] += both[sources:, LANES:]
    lead_move.wait()
    for block in range(blocks):
        at = slice(block * VS_DEV, (block + 1) * VS_DEV)
        real, imag = total[0, at, :], total[1, at, :]
        for group in range(groups):
            cosine, sine = lead_ref[group : group + 1, :], lead_ref[groups + group : groups + group + 1, :]
            out_ref[block * groups + group] = jnp.concatenate(
                [real * cosine - imag * sine, real * sine + imag * cosine], axis=1
            ).astype(jnp.bfloat16)


def pairs(got, lead):
    blocks, groups = got.shape[0], lead.shape[1] // 2
    sources, rows = blocks * VS_DEV, blocks * STEPS * STA * STA * 7 // 12
    return pl.pallas_call(
        pair_kernel,
        out_shape=pltpu.VMEM((blocks * groups, VS_DEV, 2 * LANES), jnp.bfloat16),
        in_specs=[VMEM, pl.BlockSpec(memory_space=pltpu.HBM)],
        out_specs=VMEM,
        compiler_params=pltpu.CompilerParams(vmem_limit_bytes=KERNEL_VMEM),
        scratch_shapes=[
            pltpu.VMEM(lead.shape[1:], lead.dtype),
            pltpu.VMEM((blocks, SPEC_TILES * WIN + STA, LANES), jnp.float32),
            pltpu.VMEM((blocks * WIN + STA, LANES), jnp.float32),
            pltpu.VMEM((blocks, 3 * WIN, STA, LANES), jnp.float32),
            pltpu.VMEM((blocks, 3 * WIN, STA, LANES), jnp.float32),
            pltpu.VMEM((STEPS, blocks, LANES), jnp.float32),
            pltpu.VMEM((rows, 2 * LANES), jnp.bfloat16),
            pltpu.VMEM((2 * sources, rows), jnp.bfloat16),
            pltpu.VMEM((2, sources, LANES), jnp.float32),
            pltpu.SemaphoreType.DMA,
        ],
    )(got, pltpu.with_memory_space_constraint(lead, pltpu.HBM))


def lag_kernel(bins_ref, wave_ref, turn_ref, out_ref):
    chunks = bins_ref.shape[0]
    rows = bins_ref[...].reshape(chunks * VS_DEV, 2 * LANES)
    twice = [jnp.concatenate([rows[:, part * LANES : (part + 1) * LANES]] * 2, axis=1) for part in range(2)]
    tiles = wave_ref.shape[0]
    mirror = LANES - 1 - lax.broadcasted_iota(jnp.int32, (VS_DEV, LANES), 1)
    for tile in range(tiles):
        real, imag = [jnp.dot(each, wave_ref[tile], preferred_element_type=jnp.float32) for each in twice]
        even, odd = jnp.zeros((VS_DEV, LANES), jnp.float32), jnp.zeros((VS_DEV, LANES), jnp.float32)
        for chunk in range(chunks):
            at = slice(chunk * VS_DEV, (chunk + 1) * VS_DEV)
            cosine, sine = turn_ref[0, chunk : chunk + 1, :], turn_ref[1, chunk : chunk + 1, :]
            even += real[at, :LANES] * cosine - real[at, LANES:] * sine
            odd += imag[at, :LANES] * sine + imag[at, LANES:] * cosine
        after, before = tiles + tile, tiles - 1 - tile
        out_ref[:, after * LANES : (after + 1) * LANES] = even - odd
        out_ref[:, before * LANES : (before + 1) * LANES] = jnp.take_along_axis(even + odd, mirror, axis=1)


def lags_of(bins, wave, turn):
    return pl.pallas_call(
        lag_kernel,
        out_shape=jax.ShapeDtypeStruct((VS_DEV, 2 * wave.shape[0] * LANES), jnp.float32),
        in_specs=[VMEM] * 3,
        out_specs=VMEM,
        compiler_params=pltpu.CompilerParams(vmem_limit_bytes=KERNEL_VMEM),
    )(bins, wave, turn)


def turns(phase):
    angle = np.mod(phase, 2 * BINS) * (math.pi / BINS)
    return np.cos(angle), np.sin(angle)


def lag_tables(blocks, groups):
    lag_dev = LAGS // groups
    chunks = blocks * groups
    middle = np.arange(groups) * lag_dev - LAGS // 2 + (lag_dev - 1) / 2
    bins = np.arange(LANES)
    whole = LANES * np.arange(chunks)[:, None, None] + bins
    lead = np.concatenate(turns(whole * middle[:, None]), axis=1).astype(np.float32)
    tiles = []
    for first in range(0, lag_dev // 2, LANES):
        tiles.append(np.concatenate(turns(bins[:, None] * (first + bins + 0.5)), axis=1))
    wave = np.stack(tiles) / math.sqrt(BINS)
    high = wave.astype(jnp.bfloat16)
    low = (wave - high.astype(np.float64)).astype(jnp.bfloat16)
    place = np.arange(chunks)
    chunk = place % groups * blocks + place // groups
    turn = np.stack(turns(LANES * chunk[:, None] * (bins + 0.5))).astype(np.float32)
    return jnp.asarray(lead), jnp.asarray(np.concatenate([high, low], axis=1)), jnp.asarray(turn)


def by_bins(spectra, quality, pair_mask, owners, local_rows):
    blocks, groups = lax.axis_size("blk"), lax.axis_size("grp")
    lead, wave, turn = lag_tables(blocks, groups)
    sent = pack(spectra, quality, pair_mask, owners, local_rows, blocks)
    got = lax.all_to_all(sent, "blk", split_axis=0, concat_axis=0, tiled=True)
    summed = pairs(got, lead)
    bins = lax.all_to_all(summed, ("blk", "grp"), split_axis=0, concat_axis=0, tiled=True)
    return lags_of(bins, wave, turn)


def from_behind(array, axis, by):
    size = lax.axis_size(axis)
    return lax.ppermute(array, axis, [(i, (i + by) % size) for i in range(size)])


def lag_table(bins_index, total_bins, lags):
    shifts = jnp.arange(lags, dtype=jnp.int32) - lags // 2
    phase = jnp.mod(bins_index[:, None] * shifts[None, :], 2 * total_bins)
    angle = phase.astype(jnp.float32) * (math.pi / total_bins)
    factor = 1.0 / math.sqrt(total_bins)
    return jnp.concatenate([jnp.cos(angle) * factor, -jnp.sin(angle) * factor], axis=0).astype(
        jnp.bfloat16
    )


def phase_rows(own_spec, own_weight, far_spec, far_weight, sub_mask):
    near_weight = own_weight.astype(jnp.float32)[:, :, None]
    away_weight = far_weight.astype(jnp.float32)[:, :, None]
    a_real = own_spec[0].astype(jnp.float32) * near_weight
    a_imag = own_spec[1].astype(jnp.float32) * near_weight
    b_real = far_spec[0].astype(jnp.float32) * away_weight
    b_imag = far_spec[1].astype(jnp.float32) * away_weight
    cross_real = jnp.sum(a_real[:, None] * b_real[None] + a_imag[:, None] * b_imag[None], axis=2)
    cross_imag = jnp.sum(a_imag[:, None] * b_real[None] - a_real[:, None] * b_imag[None], axis=2)
    station_mask = jnp.repeat(jnp.repeat(sub_mask, SUB, axis=0), SUB, axis=1).astype(jnp.float32)
    factor = station_mask[:, :, None] * lax.rsqrt(
        jnp.maximum(cross_real * cross_real + cross_imag * cross_imag, 1.0)
    )
    joined = jnp.concatenate([cross_real * factor, cross_imag * factor], axis=2).astype(
        jnp.bfloat16
    )
    return joined.reshape(STA * STA, joined.shape[2])


def by_halo(spectra, quality, pair_mask, owners, local_rows):
    bins_dev = spectra.shape[3]
    blocks = lax.axis_size("blk")
    rows_dev = owners.shape[0]
    capacity = max(2, 2 * rows_dev // blocks)
    masks = pair_mask[0]
    pieces = [None] * STEPS
    visiting = (spectra, quality)
    for offset in range(STEPS):
        visiting = from_behind((visiting[0], visiting[1]), "blk", 1)
        pieces[offset] = phase_rows(spectra, quality, visiting[0], visiting[1], masks[offset])
    rows_all = jnp.concatenate(pieces, axis=0)
    owner_flat = owners[:, 0]
    row_index = jnp.arange(rows_dev, dtype=jnp.int32)
    earlier = (owner_flat[:, None] == owner_flat[None, :]) & (
        row_index[None, :] < row_index[:, None]
    )
    position = jnp.sum(earlier.astype(jnp.int32), axis=1)
    slot_index = owner_flat * capacity + position
    sources = jnp.arange(VS_DEV, dtype=jnp.int32)
    bins_index = lax.axis_index("grp") * bins_dev + jnp.arange(bins_dev, dtype=jnp.int32)
    table = lag_table(bins_index, BINS, LAGS)
    lag_dev = LAGS // lax.axis_size("grp")
    lag_terms = lax.psum_scatter(
        lax.dot_general(
            table, rows_all, (((0,), (1,)), ((), ())), preferred_element_type=jnp.float32
        ),
        "grp",
        scatter_dimension=0,
        tiled=True,
    )
    outgoing = jnp.zeros((lag_dev, blocks * capacity), jnp.float32).at[:, slot_index].set(lag_terms)
    labels = jnp.full((1, blocks * capacity), -1, jnp.int32).at[0, slot_index].set(local_rows)
    received, got_labels = (
        lax.all_to_all(outgoing, "blk", split_axis=1, concat_axis=1, tiled=True),
        lax.all_to_all(labels, "blk", split_axis=1, concat_axis=1, tiled=True),
    )
    selector = (got_labels == sources[:, None]).astype(jnp.float32)
    stack = lax.dot_general(
        selector,
        received,
        (((1,), (1,)), ((), ())),
        precision=lax.Precision.HIGHEST,
        preferred_element_type=jnp.float32,
    )
    return stack


def on_device(spectra, quality, pair_mask, owners, local_rows):
    blocks, groups = lax.axis_size("blk"), lax.axis_size("grp")
    whole_tiles = spectra.shape[3] == blocks * LANES and LAGS // groups % (2 * LANES) == 0
    if whole_tiles and blocks == STEPS + 2:
        return by_bins(spectra, quality, pair_mask, owners, local_rows)
    return by_halo(spectra, quality, pair_mask, owners, local_rows)


def solution(mesh):
    in_specs = (
        P(None, "blk", None, "grp"),
        P("blk", None),
        P("blk", None, None, None),
        P("blk", None),
        P("blk"),
    )
    out_specs = P("blk", "grp")
    return jax.shard_map(
        on_device, mesh=mesh, in_specs=in_specs, out_specs=out_specs, check_vma=False
    )
```
